256 devices in a mesh: layer: 4 (over z_hi, core), query: 4 (over z_lo), doc: 16 (over y, x).
Axes of the slice: x: 4, y: 4, z: 8 (z_hi: 2, z_lo: 4; z = z_hi * 4 + z_lo), core: 2. Of those that a mesh axis runs over, the one named last changes fastest.
Arguments:
- query_out: bfloat16 [256, 11008], P(None, 'doc'), may hold values from -0.21875 to 0.21875
- query_in: bfloat16 [256, 4096], P(None, 'doc'), may hold values from -0.21875 to 0.21875
- basis_out: bfloat16 [11008, 11008], P('doc', 'layer'), may hold values from -0.0546875 to 0.0546875
- basis_in: bfloat16 [4096, 4096], P('doc', 'query'), may hold values from -0.09375 to 0.09375
- eigenvalues: bfloat16 [11008, 4096], P('layer', ('query', 'doc')), may hold values from 0.049804688 to 5
- doc_out: bfloat16 [64, 64, 11008], P('doc', None, 'layer'), may hold values from -0.21875 to 0.21875
- doc_in: bfloat16 [64, 64, 4096], P('doc', None, 'query'), may hold values from -0.21875 to 0.21875
- pair_list: int32 [64, 2], P('doc'), may hold values from 0 to 3, as said below
- pair_count: int32 [16], P('doc'), may hold values from 1 to 4, as said below
Outputs:
- scores: float32 [64, 4], P('doc')
The draws below stay inside these ranges and needn't reach their ends.
Inputs may be any that keep to these rules, and one draw needn't show every extreme that they name: `pair_list`: A row of a doc device's list is live when its position is below that device's count; column 0 is a query block below 4, column 1 one of the device's own 4 blocks; rows past the count hold ids in the same ranges and are ignored. `pair_count`: one doc device holds exactly 4 live slots in every draw.
All inputs are finite; a program needn't handle non-finite values.
Results may differ from the reference program's by a relative error of at most 0.0063.
Values may be sent and summed in bfloat16 or wider, within the bound.
No kernel may reach another device: no remote copies, remote signals or barrier semaphores. Data moves between devices by JAX's collectives and lax.ppermute only.
A program may use at most 128 MiB of HBM per device.

```python
import math
import jax
import jax.numpy as jnp
from jax import lax

FF_WIDTH = 11008
MODEL_WIDTH = 4096
FACTOR_RANK = 32
QUERY_BLOCK = 2
DOC_BLOCK = 2
SLOTS_DEV = 4
BLOCKS_DEV = 4
QUERY_ROWS = 256
QUERY_BLOCKS = 4
DOC_BLOCKS = 64
PAIR_SLOTS = 64


def draw_pair_list(key, part):
    key = jax.random.fold_in(key, 11)
    first_key, second_key = jax.random.split(key)
    query_column = jax.random.randint(first_key, (PAIR_SLOTS, 1), 0, QUERY_BLOCKS)
    block_column = jax.random.randint(second_key, (PAIR_SLOTS, 1), 0, BLOCKS_DEV)
    return jnp.concatenate([query_column, block_column], axis=1).astype(jnp.int32)


def draw_pair_count(key, part):
    key = jax.random.fold_in(key, 23)
    first_key, second_key = jax.random.split(key)
    groups = PAIR_SLOTS // SLOTS_DEV
    counts = jax.random.randint(first_key, (groups,), 1, SLOTS_DEV // 2 + 1)
    busiest = jax.random.randint(second_key, (), 0, groups)
    return jnp.where(jnp.arange(groups) == busiest, SLOTS_DEV, counts).astype(jnp.int32)


def shard_levels(rng, shape, cuts, smallest, high):
    def one(position, parts):
        steps = jax.random.uniform(jax.random.fold_in(jax.random.fold_in(rng, 6), position), (parts,), jnp.float32, smallest / len(cuts), high / len(cuts))
        return jnp.repeat(jnp.exp(steps), shape[position] // parts).reshape((-1,) + (1,) * (len(shape) - position - 1))

    level = one(*cuts[0])
    for cut in cuts[1:]:
        level = level * one(*cut)
    return level


def gaussian(own_key, dims, width, bound, pieces=(), kind=jnp.bfloat16):
    factor_of = shard_levels(own_key, dims, pieces, -0.22, 0.18) if pieces else 1.0
    array = jax.random.normal(own_key, dims, jnp.float32) * width * factor_of
    return jnp.minimum(jnp.maximum(array, -bound), bound).astype(kind)


def setup_inputs(seed: int = 0) -> dict:
    streams_of = jax.random.split(jax.random.key(seed), 10)
    return {
        "query_out": gaussian(streams_of[0], (QUERY_ROWS, FF_WIDTH), 0.034, 0.21875, ((1, 16),)),
        "query_in": gaussian(streams_of[1], (QUERY_ROWS, MODEL_WIDTH), 0.034, 0.21875, ((1, 16),)),
        "basis_out": gaussian(streams_of[2], (FF_WIDTH, FF_WIDTH), FF_WIDTH ** -0.5, 0.0546875, ((0, 16), (1, 4))),
        "basis_in": gaussian(streams_of[3], (MODEL_WIDTH, MODEL_WIDTH), MODEL_WIDTH ** -0.5, 0.09375, ((0, 16), (1, 4))),
        "eigenvalues": jnp.clip(jnp.exp(math.log(5.0) - 4.609084 * jax.random.uniform(streams_of[4], (FF_WIDTH, MODEL_WIDTH), jnp.float32) ** shard_levels(streams_of[4], (FF_WIDTH, MODEL_WIDTH), ((0, 4), (1, 64)), -0.2, 0.2)), 0.049804688, 5.0).astype(jnp.bfloat16),
        "doc_out": gaussian(streams_of[5], (DOC_BLOCKS, DOC_BLOCK * FACTOR_RANK, FF_WIDTH), 0.034, 0.21875, ((0, 16), (2, 4))),
        "doc_in": gaussian(streams_of[6], (DOC_BLOCKS, DOC_BLOCK * FACTOR_RANK, MODEL_WIDTH), 0.034, 0.21875, ((0, 16), (2, 4))),
        "pair_list": draw_pair_list(jax.random.fold_in(streams_of[9], 71), 0),
        "pair_count": draw_pair_count(jax.random.fold_in(streams_of[9], 71), 0),
    }


damping = 0.1


def reference(query_out, query_in, basis_out, basis_in, eigenvalues, doc_out, doc_in, pair_list, pair_count):
    rotated_out = jnp.dot(query_out, basis_out, preferred_element_type=jnp.float32).astype(jnp.bfloat16)
    rotated_in = jnp.dot(query_in, basis_in, preferred_element_type=jnp.float32).astype(jnp.bfloat16)
    weights = 1.0 / (eigenvalues.astype(jnp.float32) + damping)
    block_rows = QUERY_BLOCK * FACTOR_RANK

    def score_slot(slot_index):
        group = slot_index // SLOTS_DEV
        within = slot_index % SLOTS_DEV
        chosen_query = pair_list[slot_index, 0].astype(jnp.int32)
        chosen_block = (group * BLOCKS_DEV + pair_list[slot_index, 1]).astype(jnp.int32)

        def compute(unused):
            q_out = lax.dynamic_slice_in_dim(rotated_out, chosen_query * block_rows, block_rows, 0)
            q_out = q_out.astype(jnp.float32).reshape(QUERY_BLOCK, FACTOR_RANK, FF_WIDTH)
            q_in = lax.dynamic_slice_in_dim(rotated_in, chosen_query * block_rows, block_rows, 0)
            q_in = q_in.astype(jnp.float32).reshape(QUERY_BLOCK, FACTOR_RANK, MODEL_WIDTH)
            precond = (jnp.einsum("qri,qrj->qij", q_out, q_in) * weights).astype(jnp.bfloat16)
            d_out = lax.dynamic_index_in_dim(doc_out, chosen_block, 0, keepdims=False)
            d_out = d_out.astype(jnp.float32).reshape(DOC_BLOCK, FACTOR_RANK, FF_WIDTH)
            d_in = lax.dynamic_index_in_dim(doc_in, chosen_block, 0, keepdims=False)
            d_in = d_in.astype(jnp.float32).reshape(DOC_BLOCK, FACTOR_RANK, MODEL_WIDTH)
            doc_matrix = jnp.einsum("dri,drj->dij", d_out, d_in).astype(jnp.bfloat16)
            result = jnp.einsum("qij,dij->qd", precond.astype(jnp.float32), doc_matrix.astype(jnp.float32))
            return result.reshape(QUERY_BLOCK * DOC_BLOCK)

        def nothing(unused):
            return jnp.zeros((QUERY_BLOCK * DOC_BLOCK,), jnp.float32)

        return lax.cond(within < pair_count[group], compute, nothing, 0)

    return lax.map(score_slot, jnp.arange(PAIR_SLOTS, dtype=jnp.int32))
```

```python
import functools

import jax
import jax.numpy as jnp
from jax import lax
from jax.experimental import pallas as pl
from jax.experimental.pallas import tpu as pltpu
from jax.sharding import PartitionSpec as P

FACTOR_RANK = 32
QUERY_BLOCK = 2
DOC_BLOCK = 2
BAND = 256
TILE = 256
LANES = 128
SCALE = 4096.0

damping = 0.1


def score_kernel(
    pairs_ref, count_ref, rows_ref, band_ref, eig_ref, out_ref, in_ref, scores_ref,
    weights, doc_rows, scaled, total,
):
    step = pl.program_id(0)
    queries = rows_ref.shape[0]
    band = eig_ref.shape[0]
    width = eig_ref.shape[1]
    padded = doc_rows.shape[1]
    first = rows_ref.shape[1] - width
    block_rows = QUERY_BLOCK * FACTOR_RANK
    docs = out_ref.shape[0] * out_ref.shape[1]
    slots = pairs_ref.shape[0]
    live = count_ref[0]

    @pl.when(step == 0)
    def _():
        total[...] = jnp.zeros_like(total)
        start = width // LANES * LANES
        doc_rows[:, start:] = jnp.zeros((docs, padded - start), jnp.bfloat16)
        scaled[:, start:] = jnp.zeros((scaled.shape[0], padded - start), jnp.bfloat16)
        for block in range(out_ref.shape[0]):
            rows = slice(block * block_rows, (block + 1) * block_rows)
            doc_rows[rows, :width] = out_ref[block]

    shifted = eig_ref[...].astype(jnp.float32) + damping
    guess = pl.reciprocal(shifted, approx=True)
    weights[...] = guess * (2.0 - shifted * guess)

    band_rows = band_ref[...].astype(jnp.float32).T
    doc_side = jnp.concatenate([in_ref[block] for block in range(in_ref.shape[0])], axis=0)
    doc_side = doc_side.astype(jnp.float32).T
    lane = lax.broadcasted_iota(jnp.int32, (band, queries), 1) // FACTOR_RANK

    for block in range(queries // block_rows):
        wanted = jnp.bool_(False)
        for slot in range(slots):
            wanted = wanted | ((pairs_ref[slot, 0] == block) & (live > slot))

        @pl.when(wanted)
        def _():
            left = jnp.concatenate(
                [
                    jnp.where(lane == block * QUERY_BLOCK + q, band_rows, 0.0)
                    for q in range(QUERY_BLOCK)
                ],
                axis=0,
            ).astype(jnp.bfloat16)
            for begin in range(0, width, TILE):
                end = min(begin + TILE, width)
                product = jnp.dot(
                    left, rows_ref[:, first + begin:first + end], preferred_element_type=jnp.float32
                )
                for q in range(QUERY_BLOCK):
                    part = slice(q * band, (q + 1) * band)
                    scaled[part, begin:end] = (product[part] * weights[:, begin:end]).astype(jnp.bfloat16)
            mixed = lax.dot_general(
                scaled[...], doc_rows[...], (((1,), (1,)), ((), ())),
                preferred_element_type=jnp.float32,
            )
            for q in range(QUERY_BLOCK):
                part = mixed[q * band:(q + 1) * band] * doc_side
                row = block * QUERY_BLOCK + q
                total[row:row + 1, :] += jnp.sum(part, axis=0, keepdims=True)

    @pl.when(step == pl.num_programs(0) - 1)
    def _():
        shape = total.shape
        row = lax.broadcasted_iota(jnp.int32, shape, 0)
        column = lax.broadcasted_iota(jnp.int32, shape, 1)
        flat = scores_ref.shape
        out_row = lax.broadcasted_iota(jnp.int32, flat, 0)
        out_column = lax.broadcasted_iota(jnp.int32, flat, 1)
        result = jnp.zeros(flat, jnp.float32)
        for slot in range(slots):
            for q in range(QUERY_BLOCK):
                chosen = row == pairs_ref[slot, 0] * QUERY_BLOCK + q
                for d in range(DOC_BLOCK):
                    doc = pairs_ref[slot, 1] * DOC_BLOCK + d
                    inside = chosen & (column // FACTOR_RANK == doc) & (live > slot)
                    value = jnp.sum(jnp.where(inside, total[...], 0.0))
                    here = (out_row == slot * QUERY_BLOCK + q) & (out_column == d)
                    result = jnp.where(here, value, result)
        scores_ref[...] = result


def slot_scores(pairs, count, rows, eigen_rows, doc_out, doc_in):
    queries = rows.shape[0]
    model, width = eigen_rows.shape
    blocks, block_rows, _ = doc_out.shape
    padded = -(-width // TILE) * TILE
    out_rows = pairs.shape[0] * QUERY_BLOCK
    return pl.pallas_call(
        score_kernel,
        out_shape=jax.ShapeDtypeStruct((out_rows, LANES), jnp.float32),
        grid_spec=pltpu.PrefetchScalarGridSpec(
            num_scalar_prefetch=2,
            grid=(model // BAND,),
            in_specs=[
                pl.BlockSpec(rows.shape, lambda j, *_: (0, 0)),
                pl.BlockSpec((queries, BAND), lambda j, *_: (0, j)),
                pl.BlockSpec((BAND, width), lambda j, *_: (j, 0)),
                pl.BlockSpec(doc_out.shape, lambda j, *_: (0, 0, 0)),
                pl.BlockSpec((blocks, block_rows, BAND), lambda j, *_: (0, 0, j)),
            ],
            out_specs=pl.BlockSpec((out_rows, LANES), lambda j, *_: (0, 0)),
            scratch_shapes=[
                pltpu.VMEM((BAND, width), jnp.float32),
                pltpu.VMEM((blocks * block_rows, padded), jnp.bfloat16),
                pltpu.VMEM((QUERY_BLOCK * BAND, padded), jnp.bfloat16),
                pltpu.VMEM((queries // FACTOR_RANK, blocks * block_rows), jnp.float32),
            ],
        ),
        compiler_params=pltpu.CompilerParams(
            dimension_semantics=("arbitrary",), vmem_limit_bytes=48 * 2**20
        ),
        cost_estimate=pl.CostEstimate(
            flops=4 * model * width * 256 * 8, bytes_accessed=10 * 2**20, transcendentals=0
        ),
    )(pairs, count, rows, rows, eigen_rows, doc_out, doc_in)


def local(
    query_out, query_in, basis_out, basis_in, eigenvalues, doc_out, doc_in, pair_list, pair_count
):
    eigen_rows = lax.all_gather(eigenvalues.T, "doc", axis=0, tiled=True)
    parts = lax.axis_size("doc")
    queries = query_out.shape[0]
    share = queries // parts
    part_in = jnp.dot(query_in, basis_in, preferred_element_type=jnp.float32)
    part_out = jnp.dot(query_out, basis_out, preferred_element_type=jnp.float32)
    partial = jnp.concatenate([part_in, part_out], axis=1)
    width = partial.shape[1]
    sent = (partial * SCALE).astype(jnp.float16).reshape(parts, share, width)
    received = lax.all_to_all(sent, "doc", 0, 0)
    own = (jnp.sum(received.astype(jnp.float32), axis=0) * (1.0 / SCALE)).astype(jnp.bfloat16)
    copies = jnp.broadcast_to(own[None], (parts, share, width))
    rows = lax.all_to_all(copies, "doc", 0, 0).reshape(queries, width)
    scores = slot_scores(pair_list, pair_count, rows, eigen_rows, doc_out, doc_in)
    group = lax.axis_size("layer") * lax.axis_size("query")
    copies = jnp.broadcast_to(scores[None], (group,) + scores.shape)
    summed = jnp.sum(lax.all_to_all(copies, ("layer", "query"), 0, 0), axis=0)
    return summed[:, :DOC_BLOCK].reshape(pair_list.shape[0], QUERY_BLOCK * DOC_BLOCK)


def solution(mesh):
    in_specs = (
        P(None, "doc"),
        P(None, "doc"),
        P("doc", "layer"),
        P("doc", "query"),
        P("layer", ("query", "doc")),
        P("doc", None, "layer"),
        P("doc", None, "query"),
        P("doc", None),
        P("doc"),
    )
    out_specs = P("doc", None)
    return jax.shard_map(local, mesh=mesh, in_specs=in_specs, out_specs=out_specs, check_vma=False)
```

```python
import jax
import jax.numpy as jnp
from jax import lax
from jax.experimental import pallas as pl
from jax.experimental.pallas import tpu as pltpu
from jax.sharding import PartitionSpec as P

FACTOR_RANK = 32
QUERY_BLOCK = 2
DOC_BLOCK = 2
BAND = 512
TILE = 256
LANES = 128
SCALE = 4096.0

damping = 0.1


def score_kernel(
    pairs_ref, count_ref, halves_ref, own_ref, far_out_ref, own_in_ref, far_in_ref, eig_ref, out_ref, in_ref,
    scores_ref, weights, rows, doc_rows, scaled, total,
):
    step = pl.program_id(0)
    half = far_out_ref.shape[0]
    queries = 2 * half
    band, width = eig_ref.shape
    padded = doc_rows.shape[1]
    first = own_ref.shape[1] - width
    block_rows = QUERY_BLOCK * FACTOR_RANK
    docs = out_ref.shape[0] * out_ref.shape[1]
    slots = pairs_ref.shape[0]
    live = count_ref[0]

    @pl.when(step == 0)
    def _():
        total[...] = jnp.zeros_like(total)
        start = width // LANES * LANES
        doc_rows[:, start:] = jnp.zeros((docs, padded - start), jnp.bfloat16)
        scaled[:, start:] = jnp.zeros((scaled.shape[0], padded - start), jnp.bfloat16)
        for block in range(out_ref.shape[0]):
            part = slice(block * block_rows, (block + 1) * block_rows)
            doc_rows[part, :width] = out_ref[block]
        mine = pl.multiple_of(halves_ref[0] * half, half)
        rows[pl.ds(mine, half), :] = own_ref[:, first:]
        rows[pl.ds(half - mine, half), :] = far_out_ref[...]

    shifted = eig_ref[...].astype(jnp.float32) + damping
    guess = pl.reciprocal(shifted, approx=True)
    weights[...] = guess * (2.0 - shifted * guess)

    near = own_in_ref[...].astype(jnp.float32)
    far = far_in_ref[...].astype(jnp.float32)
    low = halves_ref[1] == 0
    band_rows = jnp.concatenate([jnp.where(low, near, far), jnp.where(low, far, near)], axis=0).T
    doc_side = jnp.concatenate([in_ref[block] for block in range(in_ref.shape[0])], axis=0)
    doc_side = doc_side.astype(jnp.float32).T
    lane = lax.broadcasted_iota(jnp.int32, (band, queries), 1) // FACTOR_RANK

    @pl.loop(0, queries // block_rows)
    def _(block):
        wanted = jnp.bool_(False)
        for slot in range(slots):
            wanted = wanted | ((pairs_ref[slot, 0] == block) & (live > slot))

        @pl.when(wanted)
        def _():
            left = jnp.concatenate(
                [
                    jnp.where(lane == block * QUERY_BLOCK + q, band_rows, 0.0)
                    for q in range(QUERY_BLOCK)
                ],
                axis=0,
            ).astype(jnp.bfloat16)
            for begin in range(0, width, TILE):
                end = min(begin + TILE, width)
                product = jnp.dot(left, rows[:, begin:end], preferred_element_type=jnp.float32)
                for q in range(QUERY_BLOCK):
                    part = slice(q * band, (q + 1) * band)
                    scaled[part, begin:end] = (product[part] * weights[:, begin:end]).astype(jnp.bfloat16)
            mixed = lax.dot_general(
                scaled[...], doc_rows[...], (((1,), (1,)), ((), ())),
                preferred_element_type=jnp.float32,
            )
            for q in range(QUERY_BLOCK):
                part = mixed[q * band:(q + 1) * band] * doc_side
                row = block * QUERY_BLOCK + q
                total[pl.ds(row, 1), :] += jnp.sum(part, axis=0, keepdims=True)

    @pl.when(step == pl.num_programs(0) - 1)
    def _():
        shape = total.shape
        row = lax.broadcasted_iota(jnp.int32, shape, 0)
        column = lax.broadcasted_iota(jnp.int32, shape, 1)
        flat = scores_ref.shape
        out_row = lax.broadcasted_iota(jnp.int32, flat, 0)
        out_column = lax.broadcasted_iota(jnp.int32, flat, 1)
        result = jnp.zeros(flat, jnp.float32)
        for slot in range(slots):
            for q in range(QUERY_BLOCK):
                chosen = row == pairs_ref[slot, 0] * QUERY_BLOCK + q
                for d in range(DOC_BLOCK):
                    doc = pairs_ref[slot, 1] * DOC_BLOCK + d
                    inside = chosen & (column // FACTOR_RANK == doc) & (live > slot)
                    value = jnp.sum(jnp.where(inside, total[...], 0.0))
                    here = (out_row == slot * QUERY_BLOCK + q) & (out_column == d)
                    result = jnp.where(here, value, result)
        scores_ref[...] = result


def slot_scores(pairs, count, halves, own, far_out, far_in, eigen_rows, doc_out, doc_in):
    half = own.shape[0]
    model, width = eigen_rows.shape
    blocks, block_rows, _ = doc_out.shape
    padded = -(-width // TILE) * TILE
    out_rows = pairs.shape[0] * QUERY_BLOCK
    return pl.pallas_call(
        score_kernel,
        out_shape=jax.ShapeDtypeStruct((out_rows, LANES), jnp.float32),
        grid_spec=pltpu.PrefetchScalarGridSpec(
            num_scalar_prefetch=3,
            grid=(model // BAND,),
            in_specs=[
                pl.BlockSpec(own.shape, lambda j, *_: (0, 0)),
                pl.BlockSpec(far_out.shape, lambda j, *_: (0, 0)),
                pl.BlockSpec((half, BAND), lambda j, *_: (0, j)),
                pl.BlockSpec((half, BAND), lambda j, *_: (0, j)),
                pl.BlockSpec((BAND, width), lambda j, *_: (j, 0)),
                pl.BlockSpec(doc_out.shape, lambda j, *_: (0, 0, 0)),
                pl.BlockSpec((blocks, block_rows, BAND), lambda j, *_: (0, 0, j)),
            ],
            out_specs=pl.BlockSpec((out_rows, LANES), lambda j, *_: (0, 0)),
            scratch_shapes=[
                pltpu.VMEM((BAND, width), jnp.float32),
                pltpu.VMEM((2 * half, width), jnp.bfloat16),
                pltpu.VMEM((blocks * block_rows, padded), jnp.bfloat16),
                pltpu.VMEM((QUERY_BLOCK * BAND, padded), jnp.bfloat16),
                pltpu.VMEM((2 * half // FACTOR_RANK, blocks * block_rows), jnp.float32),
            ],
        ),
        compiler_params=pltpu.CompilerParams(
            dimension_semantics=("arbitrary",), vmem_limit_bytes=48 * 2**20
        ),
        cost_estimate=pl.CostEstimate(
            flops=4 * model * width * 256 * 8, bytes_accessed=10 * 2**20, transcendentals=0
        ),
    )(pairs, count, halves, own, far_out, own, far_in, eigen_rows, doc_out, doc_in)


def local(
    query_out, query_in, basis_out, basis_in, eigenvalues, doc_out, doc_in, pair_list, pair_count
):
    eigen_rows = lax.all_gather(eigenvalues.T, "doc", axis=0, tiled=True)
    parts = lax.axis_size("doc")
    half = query_out.shape[0] // 2
    share = half // parts
    halves = jnp.stack([lax.axis_index("query") % 2, lax.axis_index("layer") % 2]).astype(jnp.int32)
    part_in = jnp.dot(
        lax.dynamic_slice_in_dim(query_in, halves[1] * half, half, 0), basis_in,
        preferred_element_type=jnp.float32,
    )
    part_out = jnp.dot(
        lax.dynamic_slice_in_dim(query_out, halves[0] * half, half, 0), basis_out,
        preferred_element_type=jnp.float32,
    )
    partial = jnp.concatenate([part_in, part_out], axis=1)
    width = partial.shape[1]
    first = part_in.shape[1]
    sent = (partial * SCALE).astype(jnp.float16).reshape(parts, share, width)
    received = lax.all_to_all(sent, "doc", 0, 0)
    summed = (jnp.sum(received.astype(jnp.float32), axis=0) * (1.0 / SCALE)).astype(jnp.bfloat16)
    copies = jnp.broadcast_to(summed[None], (parts, share, width))
    own = lax.all_to_all(copies, "doc", 0, 0).reshape(half, width)
    swap = lambda axis: [(i, i ^ 1) for i in range(lax.axis_size(axis))]
    far_out = lax.ppermute(own[:, first:], "query", swap("query"))
    far_in = lax.ppermute(own[:, :first], "layer", swap("layer"))
    scores = slot_scores(
        pair_list, pair_count, halves, own, far_out, far_in, eigen_rows, doc_out, doc_in
    )
    group = lax.axis_size("layer") * lax.axis_size("query")
    copies = jnp.broadcast_to(scores[None], (group,) + scores.shape)
    total = jnp.sum(lax.all_to_all(copies, ("layer", "query"), 0, 0), axis=0)
    return total[:, :DOC_BLOCK].reshape(pair_list.shape[0], QUERY_BLOCK * DOC_BLOCK)


def solution(mesh):
    in_specs = (
        P(None, "doc"),
        P(None, "doc"),
        P("doc", "layer"),
        P("doc", "query"),
        P("layer", ("query", "doc")),
        P("doc", None, "layer"),
        P("doc", None, "query"),
        P("doc", None),
        P("doc"),
    )
    out_specs = P("doc", None)
    return jax.shard_map(local, mesh=mesh, in_specs=in_specs, out_specs=out_specs, check_vma=False)
```

```python
import jax
import jax.numpy as jnp
from jax import lax
from jax.experimental import pallas as pl
from jax.experimental.pallas import tpu as pltpu
from jax.sharding import PartitionSpec as P

FACTOR_RANK = 32
QUERY_BLOCK = 2
DOC_BLOCK = 2
TILE = 256
LANES = 128
SIDE = 4
SCALE = 4096.0

damping = 0.1

BLOCKS, GROUPS, MINE, WANTED, QUERIES, DOCS, LIVE, SWAP, ORDER = 0, 4, 8, 9, 10, 14, 18, 19, 20


def arrange_kernel(plan, near_ref, far_ref, rows_ref, columns, *, swap):
    near = near_ref[...].astype(jnp.float32).T
    far = far_ref[...].astype(jnp.float32).T
    half = near.shape[1]
    if swap:
        keep = plan[SWAP] == 0
        near, far = jnp.where(keep, near, far), jnp.where(keep, far, near)
    columns[:, :half] = near
    columns[:, half:] = far
    count = SIDE * SIDE
    size = columns.shape[0] // count
    for place in range(count):
        source = pl.multiple_of(plan[ORDER + place] * size, size)
        rows_ref[place * size:(place + 1) * size, :] = columns[pl.ds(source, size), :].astype(jnp.bfloat16)


def arrange(plan, near, far, near_map, far_map, model, swap):
    half = 2 * FACTOR_RANK * QUERY_BLOCK
    return pl.pallas_call(
        lambda *refs: arrange_kernel(*refs, swap=swap),
        out_shape=jax.ShapeDtypeStruct((model, 2 * half), jnp.bfloat16),
        grid_spec=pltpu.PrefetchScalarGridSpec(
            num_scalar_prefetch=1,
            grid=(1,),
            in_specs=[pl.BlockSpec((half, model), near_map), pl.BlockSpec((half, model), far_map)],
            out_specs=pl.BlockSpec((model, 2 * half), lambda i, plan: (0, 0)),
            scratch_shapes=[pltpu.VMEM((model, 2 * half), jnp.float32)],
        ),
        compiler_params=pltpu.CompilerParams(vmem_limit_bytes=32 * 2**20),
        cost_estimate=pl.CostEstimate(flops=0, bytes_accessed=4 * model * half * 2, transcendentals=0),
    )(plan, near, far)


def score_kernel(plan, *refs, spread, last):
    own_ref, refs = refs[0], refs[1:]
    if last:
        far_ref, earlier_ref, refs = refs[0], refs[1], refs[2:]
    query_ref, doc_ref, doc_rows_ref = refs[:3]
    weight_refs = refs[3:3 + len(spread)]
    result_ref, weights, scaled, total, sems = refs[3 + len(spread):8 + len(spread)]
    step = pl.program_id(0)
    padded = doc_rows_ref.shape[1]
    first = own_ref.shape[1] - padded
    band = weights.shape[1]
    bands = max(spread) + 1
    if last:
        rows, first, half = refs[-1], 0, own_ref.shape[0]
        begin_place = jnp.where(step < bands - 1, plan[MINE], 0)
        end_place = plan[WANTED]
    else:
        rows, begin_place, end_place = own_ref, 0, plan[MINE]

    def fetch(which, start):
        offset = 0
        for number, place in enumerate(spread):
            if place == which:
                size = weight_refs[number].shape[0]
                copy = pltpu.make_async_copy(
                    weight_refs[number], weights.at[which % 2, pl.ds(offset, size)], sems.at[number]
                )
                copy.start() if start else copy.wait()
                offset += size

    @pl.when(step == 0)
    def _():
        fetch(0, True)
        if last:
            total[...] = earlier_ref[...]
            rows[:half] = own_ref[:, own_ref.shape[1] - padded:]
            rows[half:] = far_ref[...]
        else:
            total[...] = jnp.zeros_like(total)

    for which in range(bands):
        @pl.when(step == which)
        def _():
            fetch(which, False)
            if which + 1 < bands:
                fetch(which + 1, True)

    slot = lax.rem(step, 2)
    query_side = query_ref[...]
    doc_side = doc_ref[...].astype(jnp.float32)
    lane = lax.broadcasted_iota(jnp.int32, query_side.shape, 1) // FACTOR_RANK
    empty = jnp.zeros_like(query_side)

    @pl.loop(begin_place, end_place)
    def _(place):
        block = plan[BLOCKS + place]
        left = jnp.concatenate(
            [
                jnp.where(lane == plan[GROUPS + place] + q, query_side, empty)
                for q in range(QUERY_BLOCK)
            ],
            axis=0,
        )
        for begin in range(0, padded, TILE):
            end = begin + TILE
            product = jnp.dot(
                left, rows[:, first + begin:first + end], preferred_element_type=jnp.float32
            )
            for q in range(QUERY_BLOCK):
                part = slice(q * band, (q + 1) * band)
                scaled[part, begin:end] = (product[part] * weights[slot, :, begin:end]).astype(jnp.bfloat16)
        mixed = lax.dot_general(
            scaled[...], doc_rows_ref[...], (((1,), (1,)), ((), ())), preferred_element_type=jnp.float32,
        )
        for q in range(QUERY_BLOCK):
            part = mixed[q * band:(q + 1) * band] * doc_side
            row = block * QUERY_BLOCK + q
            total[pl.ds(row, 1), :] += jnp.sum(part, axis=0, keepdims=True)

    @pl.when(step == bands - 1)
    def _():
        if not last:
            result_ref[...] = total[...]
            return
        sums = total[...]
        row = lax.broadcasted_iota(jnp.int32, sums.shape, 0)
        doc = lax.broadcasted_iota(jnp.int32, sums.shape, 1) // FACTOR_RANK
        query = jnp.full(sums.shape, -1, jnp.int32)
        block = jnp.full(sums.shape, -1, jnp.int32)
        for number in range(sums.shape[0] // QUERY_BLOCK):
            here = (row // QUERY_BLOCK == number) & (plan[LIVE] > number)
            query = jnp.where(here, plan[QUERIES + number] * QUERY_BLOCK + row % QUERY_BLOCK, query)
            block = jnp.where(here, plan[DOCS + number], block)
        picked = jnp.zeros_like(sums)
        for number in range(sums.shape[0]):
            picked = jnp.where(query == number, sums[number:number + 1], picked)
        column = lax.broadcasted_iota(jnp.int32, result_ref.shape, 1)
        result = jnp.zeros(result_ref.shape, jnp.float32)
        for d in range(DOC_BLOCK):
            value = jnp.sum(
                jnp.where(doc == block * DOC_BLOCK + d, picked, 0.0), axis=1, keepdims=True
            )
            result = jnp.where(column == d, value, result)
        result_ref[...] = result


def slot_scores(plan, own, query_side, doc_side, doc_rows, weights, spread, rest=()):
    model, queries = query_side.shape
    docs = doc_side.shape[1]
    last = bool(rest)
    padded = doc_rows.shape[1]
    bands = max(spread) + 1
    band = sum(rows.shape[0] for rows, place in zip(weights, spread) if place == 0)
    lanes = queries if last else queries // 2
    out_rows = queries // FACTOR_RANK
    whole = lambda array: pl.BlockSpec(array.shape, lambda j, plan: (0, 0))
    in_specs = [whole(array) for array in (own, *rest)] + [
        pl.BlockSpec((band, lanes), lambda j, plan: (j, 0)),
        pl.BlockSpec((band, docs), lambda j, plan: (j, 0)),
        whole(doc_rows),
    ] + [pl.BlockSpec(memory_space=pltpu.HBM)] * len(weights)
    shape = (out_rows, LANES if last else docs)
    scratch = [
        pltpu.VMEM((2, band, padded), jnp.float32),
        pltpu.VMEM((QUERY_BLOCK * band, padded), jnp.bfloat16),
        pltpu.VMEM((out_rows, docs), jnp.float32),
        pltpu.SemaphoreType.DMA((len(weights),)),
    ]
    if last:
        scratch.append(pltpu.VMEM((queries, padded), jnp.bfloat16))
    return pl.pallas_call(
        lambda *refs: score_kernel(*refs, spread=spread, last=last),
        out_shape=jax.ShapeDtypeStruct(shape, jnp.float32),
        grid_spec=pltpu.PrefetchScalarGridSpec(
            num_scalar_prefetch=1,
            grid=(bands,),
            in_specs=in_specs,
            out_specs=pl.BlockSpec(shape, lambda j, plan: (0, 0)),
            scratch_shapes=scratch,
        ),
        compiler_params=pltpu.CompilerParams(
            dimension_semantics=("arbitrary",), vmem_limit_bytes=40 * 2**20
        ),
        cost_estimate=pl.CostEstimate(
            flops=2 * 2 * 2 * QUERY_BLOCK * bands * band * queries * padded,
            bytes_accessed=4 * bands * band * padded + 4 * 2**20, transcendentals=0,
        ),
    )(plan, own, *rest, query_side, doc_side, doc_rows, *weights)


def make_plan(pair_list, pair_count, blocks, half, swap, order):
    slots = pair_list.shape[0]
    number = jnp.arange(blocks, dtype=jnp.int32)
    names = (number + half * (blocks // 2)) % blocks
    live = jnp.arange(slots, dtype=jnp.int32) < pair_count[0]
    chosen = pair_list[:, 0]
    wanted = jnp.any(live[:, None] & (chosen[:, None] == names[None]), axis=0)
    ones = wanted.astype(jnp.int32)
    place = jnp.sum(jnp.where(number[None] < number[:, None], ones[None], 0), axis=1)
    here = wanted[None] & (place[None] == number[:, None])
    listed = jnp.sum(jnp.where(here, names[None], 0), axis=1)
    groups = jnp.sum(jnp.where(here, number[None], 0), axis=1) * QUERY_BLOCK
    mine = jnp.sum(ones[:blocks // 2])[None]
    total = jnp.sum(ones)[None]
    return jnp.concatenate(
        [listed, groups, mine, total, chosen, pair_list[:, 1], pair_count, swap[None], order]
    ).astype(jnp.int32)


def local(
    query_out, query_in, basis_out, basis_in, eigenvalues, doc_out, doc_in, pair_list, pair_count
):
    layer, query, doc = (lax.axis_index(axis) for axis in ("layer", "query", "doc"))
    parts = lax.axis_size("doc")
    core = layer % 2
    odd = query % 2
    y, x = doc // SIDE, doc % SIDE
    model = doc_in.shape[2]

    def shift(array, by, first):
        pairs = []
        for source in range(lax.axis_size("layer") * parts):
            at, (row, column) = source // parts, divmod(source % parts, SIDE)
            if (at % 2 == 0) == first:
                column = (column + by) % SIDE
            else:
                row = (row + by) % SIDE
            pairs.append((source, at * parts + row * SIDE + column))
        return lax.ppermute(array, ("layer", "doc"), pairs)

    steps = jnp.array([0, -1, 1, 2], jnp.int32)
    near = (jnp.where(core == 0, x, y) + steps) % SIDE
    far = (jnp.where(core == 0, y, x) + steps) % SIDE
    order = jnp.where(
        core == 0, far[:, None] * SIDE + near[None], near[None] * SIDE + far[:, None]
    ).reshape(-1)
    blocks = query_out.shape[0] // (QUERY_BLOCK * FACTOR_RANK)
    plan = make_plan(pair_list, pair_count, blocks, odd, (core != odd).astype(jnp.int32), order)

    tail = -eigenvalues.shape[0] % TILE
    own_rows = eigenvalues.T
    left, right, across = (shift(own_rows, by, True) for by in (1, -1, 2))
    merge = lambda *rows: jnp.pad(
        jnp.concatenate(rows, axis=0), ((0, 0), (0, tail)), constant_values=1
    )
    top, bottom = merge(own_rows, left), merge(right, across)

    half = query_out.shape[0] // 2
    share = half // parts
    part_in = jnp.dot(
        lax.dynamic_slice_in_dim(query_in, core * half, half, 0), basis_in,
        preferred_element_type=jnp.float32,
    )
    part_out = jnp.dot(
        lax.dynamic_slice_in_dim(query_out, odd * half, half, 0), basis_out,
        preferred_element_type=jnp.float32,
    )
    partial = jnp.concatenate([part_in, jnp.pad(part_out, ((0, 0), (0, tail)))], axis=1)
    width = partial.shape[1]
    sent = (partial * SCALE).astype(jnp.float16).reshape(parts, share, width)
    received = lax.all_to_all(sent, "doc", 0, 0)
    summed = (jnp.sum(received.astype(jnp.float32), axis=0) * (1.0 / SCALE)).astype(jnp.bfloat16)

    doc_rows = jnp.pad(doc_out.reshape(-1, doc_out.shape[2]), ((0, 0), (0, tail)))
    in_rows = doc_in.reshape(-1, model)
    doc_side = arrange(
        plan, in_rows, in_rows, lambda i, plan: (0, 0), lambda i, plan: (1, 0), model, False
    )
    after = [shift(rows, 1, False) for rows in (top, bottom)]
    before = [shift(rows, -1, False) for rows in (top, bottom)]

    copies = jnp.broadcast_to(summed[None], (parts, share, width))
    own = lax.all_to_all(copies, "doc", 0, 0).reshape(half, width)
    swap = lambda axis: [(i, i ^ 1) for i in range(lax.axis_size(axis))]
    far_out = lax.ppermute(own[:, model:], "query", swap("query"))
    far_in = lax.ppermute(own[:, :model], "layer", swap("layer"))

    last = [shift(after[0], 1, False), shift(before[1], -1, False)]
    wait = summed[0, 0].astype(jnp.float32) * 0.0
    weights = [
        1.0 / (rows.astype(jnp.float32) + (damping + wait)) for rows in (top, bottom)
    ] + [1.0 / (rows.astype(jnp.float32) + damping) for rows in (*after, *before, *last)]
    spread = tuple(number // 2 for number in range(len(weights)))
    query_side = arrange(
        plan, own, far_in, lambda i, plan: (0, 0), lambda i, plan: (0, 0), model, True
    )
    sums = slot_scores(plan, own, query_side, doc_side, doc_rows, weights[:-2], spread[:-2])
    scores = slot_scores(
        plan, own, query_side, doc_side, doc_rows, weights, spread, (far_out, sums)
    )
    group = lax.axis_size("layer") * lax.axis_size("query")
    copies = jnp.broadcast_to(scores[None], (group,) + scores.shape)
    total = jnp.sum(lax.all_to_all(copies, ("layer", "query"), 0, 0), axis=0)
    return total[:, :DOC_BLOCK].reshape(pair_list.shape[0], QUERY_BLOCK * DOC_BLOCK)


def solution(mesh):
    in_specs = (
        P(None, "doc"),
        P(None, "doc"),
        P("doc", "layer"),
        P("doc", "query"),
        P("layer", ("query", "doc")),
        P("doc", None, "layer"),
        P("doc", None, "query"),
        P("doc", None),
        P("doc"),
    )
    out_specs = P("doc", None)
    return jax.shard_map(local, mesh=mesh, in_specs=in_specs, out_specs=out_specs, check_vma=False)
```

```python
import jax
import jax.numpy as jnp
from jax import lax
from jax.experimental import pallas as pl
from jax.experimental.pallas import tpu as pltpu
from jax.sharding import PartitionSpec as P

FACTOR_RANK = 32
QUERY_BLOCK = 2
DOC_BLOCK = 2
TILE = 256
LANES = 128
SIDE = 4
SCALE = 4096.0

damping = 0.1

ODD, CORE, ROW, COLUMN = range(4)
STEPS = (0, SIDE - 1, 1, 2)


def arrange_kernel(here, low_ref, high_ref, rows_ref, columns, *, swap):
    low = low_ref[...].astype(jnp.float32).T
    high = high_ref[...].astype(jnp.float32).T
    half = low.shape[1]
    if swap:
        keep = here[ODD] == here[CORE]
        low, high = jnp.where(keep, low, high), jnp.where(keep, high, low)
    columns[:, :half] = low
    columns[:, half:] = high
    size = columns.shape[0] // (SIDE * SIDE)
    first = here[CORE] == 0
    for outer in range(SIDE):
        for inner in range(SIDE):
            row = lax.rem(here[ROW] + jnp.where(first, STEPS[outer], STEPS[inner]), SIDE)
            column = lax.rem(here[COLUMN] + jnp.where(first, STEPS[inner], STEPS[outer]), SIDE)
            source = pl.multiple_of((row * SIDE + column) * size, size)
            place = (outer * SIDE + inner) * size
            rows_ref[place:place + size, :] = columns[pl.ds(source, size), :].astype(jnp.bfloat16)


def arrange(here, low, high, low_map, high_map, model, swap):
    half = 2 * FACTOR_RANK * QUERY_BLOCK
    return pl.pallas_call(
        lambda *refs: arrange_kernel(*refs, swap=swap),
        out_shape=jax.ShapeDtypeStruct((model, 2 * half), jnp.bfloat16),
        grid_spec=pltpu.PrefetchScalarGridSpec(
            num_scalar_prefetch=1,
            grid=(1,),
            in_specs=[pl.BlockSpec((half, model), low_map), pl.BlockSpec((half, model), high_map)],
            out_specs=pl.BlockSpec((model, 2 * half), lambda i, here: (0, 0)),
            scratch_shapes=[pltpu.VMEM((model, 2 * half), jnp.float32)],
        ),
        compiler_params=pltpu.CompilerParams(vmem_limit_bytes=32 * 2**20),
        cost_estimate=pl.CostEstimate(flops=0, bytes_accessed=4 * model * half * 2, transcendentals=0),
    )(here, low, high)


def score_kernel(pairs, count, here, *refs, spread, last):
    own_ref, refs = refs[0], refs[1:]
    if last:
        far_ref, earlier_ref, refs = refs[0], refs[1], refs[2:]
    query_ref, doc_ref, doc_rows_ref = refs[:3]
    eigen_refs = refs[3:3 + len(spread)]
    result_ref, eigen, weights, scaled, total, sems = refs[3 + len(spread):9 + len(spread)]
    step = pl.program_id(0)
    padded = doc_rows_ref.shape[1]
    first = own_ref.shape[1] - padded
    band = weights.shape[0]
    bands = max(spread) + 1
    slots = pairs.shape[1]
    blocks = total.shape[0] // QUERY_BLOCK
    if last:
        rows, first, half = refs[-1], 0, own_ref.shape[0]
        begin_place = jnp.where(step < bands - 1, blocks // 2, 0)
        end_place = blocks
    else:
        rows, begin_place, end_place = own_ref, 0, blocks // 2

    def fetch(which, start):
        offset = 0
        for number, place in enumerate(spread):
            if place == which:
                size = eigen_refs[number].shape[0]
                copy = pltpu.make_async_copy(
                    eigen_refs[number], eigen.at[which % 2, pl.ds(offset, size)], sems.at[number]
                )
                copy.start() if start else copy.wait()
                offset += size

    @pl.when(step == 0)
    def _():
        fetch(0, True)
        if last:
            total[...] = earlier_ref[...]
            rows[:half] = own_ref[:, own_ref.shape[1] - padded:]
            rows[half:] = far_ref[...]
        else:
            total[...] = jnp.zeros_like(total)

    for which in range(bands):
        @pl.when(step == which)
        def _():
            fetch(which, False)
            if which + 1 < bands:
                fetch(which + 1, True)

    shifted = eigen[lax.rem(step, 2)].astype(jnp.float32) + damping
    guess = pl.reciprocal(shifted, approx=True)
    weights[...] = guess * (2.0 - shifted * guess)
    query_side = query_ref[...]
    doc_side = doc_ref[...].astype(jnp.float32)
    lane = lax.broadcasted_iota(jnp.int32, query_side.shape, 1) // FACTOR_RANK
    empty = jnp.zeros_like(query_side)

    @pl.loop(begin_place, end_place)
    def _(place):
        block = lax.rem(place + here[ODD] * (blocks // 2), blocks)
        wanted = jnp.bool_(False)
        for slot in range(slots):
            wanted = wanted | ((pairs[0, slot] == block) & (count[0] > slot))

        @pl.when(wanted)
        def _():
            left = jnp.concatenate(
                [
                    jnp.where(lane == place * QUERY_BLOCK + q, query_side, empty)
                    for q in range(QUERY_BLOCK)
                ],
                axis=0,
            )
            for begin in range(0, padded, TILE):
                end = begin + TILE
                product = jnp.dot(
                    left, rows[:, first + begin:first + end], preferred_element_type=jnp.float32
                )
                for q in range(QUERY_BLOCK):
                    part = slice(q * band, (q + 1) * band)
                    scaled[part, begin:end] = (product[part] * weights[:, begin:end]).astype(jnp.bfloat16)
            mixed = lax.dot_general(
                scaled[...], doc_rows_ref[...], (((1,), (1,)), ((), ())),
                preferred_element_type=jnp.float32,
            )
            for q in range(QUERY_BLOCK):
                part = mixed[q * band:(q + 1) * band] * doc_side
                row = block * QUERY_BLOCK + q
                total[pl.ds(row, 1), :] += jnp.sum(part, axis=0, keepdims=True)

    @pl.when(step == bands - 1)
    def _():
        if not last:
            result_ref[...] = total[...]
            return
        sums = total[...]
        row = lax.broadcasted_iota(jnp.int32, sums.shape, 0)
        doc = lax.broadcasted_iota(jnp.int32, sums.shape, 1) // FACTOR_RANK
        query = jnp.full(sums.shape, -1, jnp.int32)
        block = jnp.full(sums.shape, -1, jnp.int32)
        for number in range(sums.shape[0] // QUERY_BLOCK):
            inside = (row // QUERY_BLOCK == number) & (count[0] > number)
            query = jnp.where(inside, pairs[0, number] * QUERY_BLOCK + row % QUERY_BLOCK, query)
            block = jnp.where(inside, pairs[1, number], block)
        picked = jnp.zeros_like(sums)
        for number in range(sums.shape[0]):
            picked = jnp.where(query == number, sums[number:number + 1], picked)
        column = lax.broadcasted_iota(jnp.int32, result_ref.shape, 1)
        result = jnp.zeros(result_ref.shape, jnp.float32)
        for d in range(DOC_BLOCK):
            value = jnp.sum(
                jnp.where(doc == block * DOC_BLOCK + d, picked, 0.0), axis=1, keepdims=True
            )
            result = jnp.where(column == d, value, result)
        result_ref[...] = result


def slot_scores(scalars, own, query_side, doc_side, doc_rows, eigen, spread, rest=()):
    model, queries = query_side.shape
    docs = doc_side.shape[1]
    last = bool(rest)
    padded = doc_rows.shape[1]
    bands = max(spread) + 1
    band = sum(rows.shape[0] for rows, place in zip(eigen, spread) if place == 0)
    lanes = queries if last else queries // 2
    out_rows = queries // FACTOR_RANK
    whole = lambda array: pl.BlockSpec(array.shape, lambda j, *_: (0, 0))
    in_specs = [whole(array) for array in (own, *rest)] + [
        pl.BlockSpec((band, lanes), lambda j, *_: (j, 0)),
        pl.BlockSpec((band, docs), lambda j, *_: (j, 0)),
        whole(doc_rows),
    ] + [pl.BlockSpec(memory_space=pl.ANY)] * len(eigen)
    shape = (out_rows, LANES if last else docs)
    scratch = [
        pltpu.VMEM((2, band, padded), jnp.bfloat16),
        pltpu.VMEM((band, padded), jnp.float32),
        pltpu.VMEM((QUERY_BLOCK * band, padded), jnp.bfloat16),
        pltpu.VMEM((out_rows, docs), jnp.float32),
        pltpu.SemaphoreType.DMA((len(eigen),)),
    ]
    if last:
        scratch.append(pltpu.VMEM((queries, padded), jnp.bfloat16))
    return pl.pallas_call(
        lambda *refs: score_kernel(*refs, spread=spread, last=last),
        out_shape=jax.ShapeDtypeStruct(shape, jnp.float32),
        grid_spec=pltpu.PrefetchScalarGridSpec(
            num_scalar_prefetch=len(scalars),
            grid=(bands,),
            in_specs=in_specs,
            out_specs=pl.BlockSpec(shape, lambda j, *_: (0, 0)),
            scratch_shapes=scratch,
        ),
        compiler_params=pltpu.CompilerParams(
            dimension_semantics=("arbitrary",), vmem_limit_bytes=40 * 2**20
        ),
        cost_estimate=pl.CostEstimate(
            flops=2 * 2 * 2 * QUERY_BLOCK * bands * band * queries * padded,
            bytes_accessed=4 * bands * band * padded + 4 * 2**20, transcendentals=0,
        ),
    )(*scalars, own, *rest, query_side, doc_side, doc_rows, *eigen)


def local(
    query_out, query_in, basis_out, basis_in, eigenvalues, doc_out, doc_in, pair_list, pair_count
):
    layer, query, doc = (lax.axis_index(axis) for axis in ("layer", "query", "doc"))
    parts = lax.axis_size("doc")
    core = layer % 2
    odd = query % 2
    y, x = doc // SIDE, doc % SIDE
    model = doc_in.shape[2]

    def shift(array, by, first):
        pairs = []
        for source in range(lax.axis_size("layer") * parts):
            at, (row, column) = source // parts, divmod(source % parts, SIDE)
            if (at % 2 == 0) == first:
                column = (column + by) % SIDE
            else:
                row = (row + by) % SIDE
            pairs.append((source, at * parts + row * SIDE + column))
        return lax.ppermute(array, ("layer", "doc"), pairs)

    here = jnp.stack([odd, core, y, x]).astype(jnp.int32)
    scalars = (pair_list.T, pair_count, here)
    tail = -eigenvalues.shape[0] % TILE
    own_rows = eigenvalues.T
    left, right, across = (shift(own_rows, by, True) for by in (1, -1, 2))
    merge = lambda *rows: jnp.pad(
        jnp.concatenate(rows, axis=0), ((0, 0), (0, tail)), constant_values=1
    )
    top, bottom = merge(own_rows, left), merge(right, across)

    half = query_out.shape[0] // 2
    share = half // parts
    part_in = jnp.dot(
        lax.dynamic_slice_in_dim(query_in, core * half, half, 0), basis_in,
        preferred_element_type=jnp.float32,
    )
    part_out = jnp.dot(
        lax.dynamic_slice_in_dim(query_out, odd * half, half, 0), basis_out,
        preferred_element_type=jnp.float32,
    )
    partial = jnp.concatenate([part_in, jnp.pad(part_out, ((0, 0), (0, tail)))], axis=1)
    width = partial.shape[1]
    sent = (partial * SCALE).astype(jnp.float16).reshape(parts, share, width)
    received = lax.all_to_all(sent, "doc", 0, 0)
    summed = (jnp.sum(received.astype(jnp.float32), axis=0) * (1.0 / SCALE)).astype(jnp.bfloat16)

    doc_rows = jnp.pad(doc_out.reshape(-1, doc_out.shape[2]), ((0, 0), (0, tail)))
    in_rows = doc_in.reshape(-1, model)
    doc_side = arrange(here, in_rows, in_rows, lambda i, _: (0, 0), lambda i, _: (1, 0), model, False)
    after = [shift(rows, 1, False) for rows in (top, bottom)]
    before = [shift(rows, -1, False) for rows in (top, bottom)]

    copies = jnp.broadcast_to(summed[None], (parts, share, width))
    own = lax.all_to_all(copies, "doc", 0, 0).reshape(half, width)
    swap = lambda axis: [(i, i ^ 1) for i in range(lax.axis_size(axis))]
    far_out = lax.ppermute(own[:, model:], "query", swap("query"))
    far_in = lax.ppermute(own[:, :model], "layer", swap("layer"))

    last = [shift(after[0], 1, False), shift(before[1], -1, False)]
    eigen = [top, bottom, *after, *before, *last]
    spread = tuple(number // 2 for number in range(len(eigen)))
    query_side = arrange(here, own, far_in, lambda i, _: (0, 0), lambda i, _: (0, 0), model, True)
    sums = slot_scores(scalars, own, query_side, doc_side, doc_rows, eigen[:-2], spread[:-2])
    scores = slot_scores(
        scalars, own, query_side, doc_side, doc_rows, eigen, spread, (far_out, sums)
    )
    group = lax.axis_size("layer") * lax.axis_size("query")
    copies = jnp.broadcast_to(scores[None], (group,) + scores.shape)
    total = jnp.sum(lax.all_to_all(copies, ("layer", "query"), 0, 0), axis=0)
    return total[:, :DOC_BLOCK].reshape(pair_list.shape[0], QUERY_BLOCK * DOC_BLOCK)


def solution(mesh):
    in_specs = (
        P(None, "doc"),
        P(None, "doc"),
        P("doc", "layer"),
        P("doc", "query"),
        P("layer", ("query", "doc")),
        P("doc", None, "layer"),
        P("doc", None, "query"),
        P("doc", None),
        P("doc"),
    )
    out_specs = P("doc", None)
    return jax.shard_map(local, mesh=mesh, in_specs=in_specs, out_specs=out_specs, check_vma=False)
```

```python
import jax
import jax.numpy as jnp
from jax import lax
from jax.experimental import pallas as pl
from jax.experimental.pallas import tpu as pltpu
from jax.sharding import PartitionSpec as P

FACTOR_RANK = 32
QUERY_BLOCK = 2
DOC_BLOCK = 2
TILE = 256
LANES = 128
SIDE = 4
SCALE = 4096.0

damping = 0.1

ODD, CORE, ROW, COLUMN = range(4)
STEPS = (0, SIDE - 1, 1, 2)


def arrange_kernel(here, low_ref, high_ref, rows_ref, columns, *, swap):
    low = low_ref[...].astype(jnp.float32).T
    high = high_ref[...].astype(jnp.float32).T
    half = low.shape[1]
    if swap:
        keep = here[ODD] == here[CORE]
        low, high = jnp.where(keep, low, high), jnp.where(keep, high, low)
    columns[:, :half] = low
    columns[:, half:] = high
    size = columns.shape[0] // (SIDE * SIDE)
    first = here[CORE] == 0
    for outer in range(SIDE):
        for inner in range(SIDE):
            row = lax.rem(here[ROW] + jnp.where(first, STEPS[outer], STEPS[inner]), SIDE)
            column = lax.rem(here[COLUMN] + jnp.where(first, STEPS[inner], STEPS[outer]), SIDE)
            source = pl.multiple_of((row * SIDE + column) * size, size)
            place = (outer * SIDE + inner) * size
            rows_ref[place:place + size, :] = columns[pl.ds(source, size), :].astype(jnp.bfloat16)


def arrange(here, low, high, low_map, high_map, model, swap):
    half = 2 * FACTOR_RANK * QUERY_BLOCK
    return pl.pallas_call(
        lambda *refs: arrange_kernel(*refs, swap=swap),
        out_shape=jax.ShapeDtypeStruct((model, 2 * half), jnp.bfloat16),
        grid_spec=pltpu.PrefetchScalarGridSpec(
            num_scalar_prefetch=1,
            grid=(1,),
            in_specs=[pl.BlockSpec((half, model), low_map), pl.BlockSpec((half, model), high_map)],
            out_specs=pl.BlockSpec((model, 2 * half), lambda i, here: (0, 0)),
            scratch_shapes=[pltpu.VMEM((model, 2 * half), jnp.float32)],
        ),
        compiler_params=pltpu.CompilerParams(vmem_limit_bytes=32 * 2**20),
        cost_estimate=pl.CostEstimate(flops=0, bytes_accessed=4 * model * half * 2, transcendentals=0),
    )(here, low, high)


def score_kernel(pairs, count, here, *refs, spread, last):
    own_ref, refs = refs[0], refs[1:]
    if last:
        far_ref, earlier_ref, refs = refs[0], refs[1], refs[2:]
    query_ref, doc_ref, doc_rows_ref = refs[:3]
    eigen_refs = refs[3:3 + len(spread)]
    result_ref, eigen, weights, scaled, total, sems = refs[3 + len(spread):9 + len(spread)]
    step = pl.program_id(0)
    padded = doc_rows_ref.shape[1]
    first = own_ref.shape[1] - padded
    band = weights.shape[0]
    bands = max(spread) + 1
    slots = pairs.shape[1]
    blocks = total.shape[0] // QUERY_BLOCK
    if last:
        rows, first, half = refs[-1], 0, own_ref.shape[0]
        begin_place = jnp.where(step < bands - 1, blocks // 2, 0)
        end_place = blocks
    else:
        rows, begin_place, end_place = own_ref, 0, blocks // 2

    def fetch(which, start):
        offset = 0
        for number, place in enumerate(spread):
            if place == which:
                size = eigen_refs[number].shape[0]
                copy = pltpu.make_async_copy(
                    eigen_refs[number], eigen.at[which % 2, pl.ds(offset, size)], sems.at[number]
                )
                copy.start() if start else copy.wait()
                offset += size

    @pl.when(step == 0)
    def _():
        fetch(0, True)
        if last:
            total[...] = earlier_ref[...]
            rows[:half] = own_ref[:, own_ref.shape[1] - padded:]
            rows[half:] = far_ref[...]
        else:
            total[...] = jnp.zeros_like(total)

    for which in range(bands):
        @pl.when(step == which)
        def _():
            fetch(which, False)
            if which + 1 < bands:
                fetch(which + 1, True)

    shifted = eigen[lax.rem(step, 2)].astype(jnp.float32) + damping
    guess = pl.reciprocal(shifted, approx=True)
    weights[...] = guess * (2.0 - shifted * guess)
    query_side = query_ref[...]
    doc_side = doc_ref[...].astype(jnp.float32)
    lane = lax.broadcasted_iota(jnp.int32, query_side.shape, 1) // FACTOR_RANK
    empty = jnp.zeros_like(query_side)

    def score(places):
        left = jnp.concatenate(
            [
                jnp.where(lane == place * QUERY_BLOCK + q, query_side, empty)
                for place in places for q in range(QUERY_BLOCK)
            ],
            axis=0,
        )
        parts = len(places) * QUERY_BLOCK
        for begin in range(0, padded, TILE):
            end = begin + TILE
            product = jnp.dot(
                left, rows[:, first + begin:first + end], preferred_element_type=jnp.float32
            )
            for q in range(parts):
                part = slice(q * band, (q + 1) * band)
                scaled[part, begin:end] = (product[part] * weights[:, begin:end]).astype(jnp.bfloat16)
        mixed = lax.dot_general(
            scaled[:parts * band], doc_rows_ref[...], (((1,), (1,)), ((), ())),
            preferred_element_type=jnp.float32,
        )
        for q in range(parts):
            part = mixed[q * band:(q + 1) * band] * doc_side
            block = lax.rem(places[q // QUERY_BLOCK] + here[ODD] * (blocks // 2), blocks)
            row = block * QUERY_BLOCK + q % QUERY_BLOCK
            total[pl.ds(row, 1), :] += jnp.sum(part, axis=0, keepdims=True)

    def wanted(place):
        block = lax.rem(place + here[ODD] * (blocks // 2), blocks)
        found = jnp.bool_(False)
        for slot in range(slots):
            found = found | ((pairs[0, slot] == block) & (count[0] > slot))
        return found

    @pl.loop(begin_place // 2, end_place // 2)
    def _(pair):
        lower, upper = wanted(2 * pair), wanted(2 * pair + 1)

        @pl.when(lower & upper)
        def _():
            score((2 * pair, 2 * pair + 1))

        @pl.when(lower != upper)
        def _():
            score((2 * pair + jnp.where(upper, 1, 0),))

    @pl.when(step == bands - 1)
    def _():
        if not last:
            result_ref[...] = total[...]
            return
        sums = total[...]
        row = lax.broadcasted_iota(jnp.int32, sums.shape, 0)
        doc = lax.broadcasted_iota(jnp.int32, sums.shape, 1) // FACTOR_RANK
        query = jnp.full(sums.shape, -1, jnp.int32)
        block = jnp.full(sums.shape, -1, jnp.int32)
        for number in range(sums.shape[0] // QUERY_BLOCK):
            inside = (row // QUERY_BLOCK == number) & (count[0] > number)
            query = jnp.where(inside, pairs[0, number] * QUERY_BLOCK + row % QUERY_BLOCK, query)
            block = jnp.where(inside, pairs[1, number], block)
        picked = jnp.zeros_like(sums)
        for number in range(sums.shape[0]):
            picked = jnp.where(query == number, sums[number:number + 1], picked)
        column = lax.broadcasted_iota(jnp.int32, result_ref.shape, 1)
        result = jnp.zeros(result_ref.shape, jnp.float32)
        for d in range(DOC_BLOCK):
            value = jnp.sum(
                jnp.where(doc == block * DOC_BLOCK + d, picked, 0.0), axis=1, keepdims=True
            )
            result = jnp.where(column == d, value, result)
        result_ref[...] = result


def slot_scores(scalars, own, query_side, doc_side, doc_rows, eigen, spread, rest=()):
    model, queries = query_side.shape
    docs = doc_side.shape[1]
    last = bool(rest)
    padded = doc_rows.shape[1]
    bands = max(spread) + 1
    band = sum(rows.shape[0] for rows, place in zip(eigen, spread) if place == 0)
    lanes = queries if last else queries // 2
    out_rows = queries // FACTOR_RANK
    whole = lambda array: pl.BlockSpec(array.shape, lambda j, *_: (0, 0))
    in_specs = [whole(array) for array in (own, *rest)] + [
        pl.BlockSpec((band, lanes), lambda j, *_: (j, 0)),
        pl.BlockSpec((band, docs), lambda j, *_: (j, 0)),
        whole(doc_rows),
    ] + [pl.BlockSpec(memory_space=pl.ANY)] * len(eigen)
    shape = (out_rows, LANES if last else docs)
    scratch = [
        pltpu.VMEM((2, band, padded), jnp.bfloat16),
        pltpu.VMEM((band, padded), jnp.float32),
        pltpu.VMEM((2 * QUERY_BLOCK * band, padded), jnp.bfloat16),
        pltpu.VMEM((out_rows, docs), jnp.float32),
        pltpu.SemaphoreType.DMA((len(eigen),)),
    ]
    if last:
        scratch.append(pltpu.VMEM((queries, padded), jnp.bfloat16))
    return pl.pallas_call(
        lambda *refs: score_kernel(*refs, spread=spread, last=last),
        out_shape=jax.ShapeDtypeStruct(shape, jnp.float32),
        grid_spec=pltpu.PrefetchScalarGridSpec(
            num_scalar_prefetch=len(scalars),
            grid=(bands,),
            in_specs=in_specs,
            out_specs=pl.BlockSpec(shape, lambda j, *_: (0, 0)),
            scratch_shapes=scratch,
        ),
        compiler_params=pltpu.CompilerParams(
            dimension_semantics=("arbitrary",), vmem_limit_bytes=40 * 2**20
        ),
        cost_estimate=pl.CostEstimate(
            flops=2 * 2 * 2 * QUERY_BLOCK * bands * band * queries * padded,
            bytes_accessed=4 * bands * band * padded + 4 * 2**20, transcendentals=0,
        ),
    )(*scalars, own, *rest, query_side, doc_side, doc_rows, *eigen)


def local(
    query_out, query_in, basis_out, basis_in, eigenvalues, doc_out, doc_in, pair_list, pair_count
):
    layer, query, doc = (lax.axis_index(axis) for axis in ("layer", "query", "doc"))
    parts = lax.axis_size("doc")
    core = layer % 2
    odd = query % 2
    y, x = doc // SIDE, doc % SIDE
    model = doc_in.shape[2]

    def shift(array, by, first):
        pairs = []
        for source in range(lax.axis_size("layer") * parts):
            at, (row, column) = source // parts, divmod(source % parts, SIDE)
            if (at % 2 == 0) == first:
                column = (column + by) % SIDE
            else:
                row = (row + by) % SIDE
            pairs.append((source, at * parts + row * SIDE + column))
        return lax.ppermute(array, ("layer", "doc"), pairs)

    here = jnp.stack([odd, core, y, x]).astype(jnp.int32)
    scalars = (pair_list.T, pair_count, here)
    tail = -eigenvalues.shape[0] % TILE
    own_rows = eigenvalues.T
    left, right, across = (shift(own_rows, by, True) for by in (1, -1, 2))
    merge = lambda *rows: jnp.pad(
        jnp.concatenate(rows, axis=0), ((0, 0), (0, tail)), constant_values=1
    )
    top, bottom = merge(own_rows, left), merge(right, across)

    half = query_out.shape[0] // 2
    share = half // parts
    part_in = jnp.dot(
        lax.dynamic_slice_in_dim(query_in, core * half, half, 0), basis_in,
        preferred_element_type=jnp.float32,
    )
    part_out = jnp.dot(
        lax.dynamic_slice_in_dim(query_out, odd * half, half, 0), basis_out,
        preferred_element_type=jnp.float32,
    )
    partial = jnp.concatenate([part_in, jnp.pad(part_out, ((0, 0), (0, tail)))], axis=1)
    width = partial.shape[1]
    sent = (partial * SCALE).astype(jnp.float16).reshape(parts, share, width)
    received = lax.all_to_all(sent, "doc", 0, 0)
    summed = (jnp.sum(received.astype(jnp.float32), axis=0) * (1.0 / SCALE)).astype(jnp.bfloat16)

    doc_rows = jnp.pad(doc_out.reshape(-1, doc_out.shape[2]), ((0, 0), (0, tail)))
    in_rows = doc_in.reshape(-1, model)
    doc_side = arrange(here, in_rows, in_rows, lambda i, _: (0, 0), lambda i, _: (1, 0), model, False)
    after = [shift(rows, 1, False) for rows in (top, bottom)]
    before = [shift(rows, -1, False) for rows in (top, bottom)]

    copies = jnp.broadcast_to(summed[None], (parts, share, width))
    own = lax.all_to_all(copies, "doc", 0, 0).reshape(half, width)
    swap = lambda axis: [(i, i ^ 1) for i in range(lax.axis_size(axis))]
    far_out = lax.ppermute(own[:, model:], "query", swap("query"))
    far_in = lax.ppermute(own[:, :model], "layer", swap("layer"))

    last = [shift(after[0], 1, False), shift(before[1], -1, False)]
    eigen = [top, bottom, *after, *before, *last]
    spread = tuple(number // 2 for number in range(len(eigen)))
    query_side = arrange(here, own, far_in, lambda i, _: (0, 0), lambda i, _: (0, 0), model, True)
    sums = slot_scores(scalars, own, query_side, doc_side, doc_rows, eigen[:-2], spread[:-2])
    scores = slot_scores(
        scalars, own, query_side, doc_side, doc_rows, eigen, spread, (far_out, sums)
    )
    group = lax.axis_size("layer") * lax.axis_size("query")
    copies = jnp.broadcast_to(scores[None], (group,) + scores.shape)
    total = jnp.sum(lax.all_to_all(copies, ("layer", "query"), 0, 0), axis=0)
    return total[:, :DOC_BLOCK].reshape(pair_list.shape[0], QUERY_BLOCK * DOC_BLOCK)


def solution(mesh):
    in_specs = (
        P(None, "doc"),
        P(None, "doc"),
        P("doc", "layer"),
        P("doc", "query"),
        P("layer", ("query", "doc")),
        P("doc", None, "layer"),
        P("doc", None, "query"),
        P("doc", None),
        P("doc"),
    )
    out_specs = P("doc", None)
    return jax.shard_map(local, mesh=mesh, in_specs=in_specs, out_specs=out_specs, check_vma=False)
```

```python
import jax
import jax.numpy as jnp
from jax import lax
from jax.experimental import pallas as pl
from jax.experimental.pallas import tpu as pltpu
from jax.sharding import PartitionSpec as P

FACTOR_RANK = 32
QUERY_BLOCK = 2
DOC_BLOCK = 2
TILE = 256
LANES = 128
SIDE = 4
SCALE = 4096.0

damping = 0.1

ODD, CORE, ROW, COLUMN = range(4)
STEPS = (0, SIDE - 1, 1, 2)


def arrange_kernel(here, low_ref, high_ref, rows_ref, columns, *, swap):
    low = low_ref[...].astype(jnp.float32).T
    high = high_ref[...].astype(jnp.float32).T
    half = low.shape[1]
    if swap:
        keep = here[ODD] == here[CORE]
        low, high = jnp.where(keep, low, high), jnp.where(keep, high, low)
    columns[:, :half] = low
    columns[:, half:] = high
    size = columns.shape[0] // (SIDE * SIDE)
    first = here[CORE] == 0
    for outer in range(SIDE):
        for inner in range(SIDE):
            row = lax.rem(here[ROW] + jnp.where(first, STEPS[outer], STEPS[inner]), SIDE)
            column = lax.rem(here[COLUMN] + jnp.where(first, STEPS[inner], STEPS[outer]), SIDE)
            source = pl.multiple_of((row * SIDE + column) * size, size)
            place = (outer * SIDE + inner) * size
            rows_ref[place:place + size, :] = columns[pl.ds(source, size), :].astype(jnp.bfloat16)


def arrange(here, low, high, low_map, high_map, model, swap):
    half = 2 * FACTOR_RANK * QUERY_BLOCK
    return pl.pallas_call(
        lambda *refs: arrange_kernel(*refs, swap=swap),
        out_shape=jax.ShapeDtypeStruct((model, 2 * half), jnp.bfloat16),
        grid_spec=pltpu.PrefetchScalarGridSpec(
            num_scalar_prefetch=1,
            grid=(1,),
            in_specs=[pl.BlockSpec((half, model), low_map), pl.BlockSpec((half, model), high_map)],
            out_specs=pl.BlockSpec((model, 2 * half), lambda i, here: (0, 0)),
            scratch_shapes=[pltpu.VMEM((model, 2 * half), jnp.float32)],
        ),
        compiler_params=pltpu.CompilerParams(vmem_limit_bytes=32 * 2**20),
        cost_estimate=pl.CostEstimate(flops=0, bytes_accessed=4 * model * half * 2, transcendentals=0),
    )(here, low, high)


def score_kernel(pairs, count, here, *refs, spread, last):
    own_ref, refs = refs[0], refs[1:]
    if last:
        far_ref, earlier_ref, refs = refs[0], refs[1], refs[2:]
    query_ref, doc_ref, doc_rows_ref = refs[:3]
    eigen_refs = refs[3:3 + len(spread)]
    result_ref, eigen, scaled, total, sems = refs[3 + len(spread):8 + len(spread)]
    step = pl.program_id(0)
    padded = doc_rows_ref.shape[1]
    first = own_ref.shape[1] - padded
    band = eigen.shape[1]
    bands = max(spread) + 1
    slots = pairs.shape[1]
    blocks = total.shape[0] // QUERY_BLOCK
    if last:
        rows, first, half = refs[-1], 0, own_ref.shape[0]
        begin_place = jnp.where(step < bands - 1, blocks // 2, 0)
        end_place = blocks
    else:
        rows, begin_place, end_place = own_ref, 0, blocks // 2

    def fetch(which, start):
        offset = 0
        for number, place in enumerate(spread):
            if place == which:
                size = eigen_refs[number].shape[0]
                copy = pltpu.make_async_copy(
                    eigen_refs[number], eigen.at[which % 2, pl.ds(offset, size)], sems.at[number]
                )
                copy.start() if start else copy.wait()
                offset += size

    @pl.when(step == 0)
    def _():
        fetch(0, True)
        if last:
            total[...] = earlier_ref[...]
            rows[:half] = own_ref[:, own_ref.shape[1] - padded:]
            rows[half:] = far_ref[...]
        else:
            total[...] = jnp.zeros_like(total)

    for which in range(bands):
        @pl.when(step == which)
        def _():
            fetch(which, False)
            if which + 1 < bands:
                fetch(which + 1, True)

    arrived = lax.rem(step, 2)
    query_side = query_ref[...]
    doc_side = doc_ref[...].astype(jnp.float32)
    lane = lax.broadcasted_iota(jnp.int32, query_side.shape, 1) // FACTOR_RANK
    empty = jnp.zeros_like(query_side)

    def score(places):
        left = jnp.concatenate(
            [
                jnp.where(lane == place * QUERY_BLOCK + q, query_side, empty)
                for place in places for q in range(QUERY_BLOCK)
            ],
            axis=0,
        )
        parts = len(places) * QUERY_BLOCK
        for begin in range(0, padded, TILE):
            end = begin + TILE
            product = jnp.dot(
                left, rows[:, first + begin:first + end], preferred_element_type=jnp.float32
            )
            shifted = eigen[arrived, :, begin:end].astype(jnp.float32) + damping
            guess = pl.reciprocal(shifted, approx=True)
            weights = guess * (2.0 - shifted * guess)
            for q in range(parts):
                part = slice(q * band, (q + 1) * band)
                scaled[part, begin:end] = (product[part] * weights).astype(jnp.bfloat16)
        mixed = lax.dot_general(
            scaled[:parts * band], doc_rows_ref[...], (((1,), (1,)), ((), ())),
            preferred_element_type=jnp.float32,
        )
        for q in range(parts):
            part = mixed[q * band:(q + 1) * band] * doc_side
            block = lax.rem(places[q // QUERY_BLOCK] + here[ODD] * (blocks // 2), blocks)
            row = block * QUERY_BLOCK + q % QUERY_BLOCK
            total[pl.ds(row, 1), :] += jnp.sum(part, axis=0, keepdims=True)

    def wanted(place):
        block = lax.rem(place + here[ODD] * (blocks // 2), blocks)
        found = jnp.bool_(False)
        for slot in range(slots):
            found = found | ((pairs[0, slot] == block) & (count[0] > slot))
        return found

    @pl.loop(begin_place // 2, end_place // 2)
    def _(pair):
        lower, upper = wanted(2 * pair), wanted(2 * pair + 1)

        @pl.when(lower & upper)
        def _():
            score((2 * pair, 2 * pair + 1))

        @pl.when(lower != upper)
        def _():
            score((2 * pair + jnp.where(upper, 1, 0),))

    @pl.when(step == bands - 1)
    def _():
        if not last:
            result_ref[...] = total[...]
            return
        sums = total[...]
        row = lax.broadcasted_iota(jnp.int32, sums.shape, 0)
        doc = lax.broadcasted_iota(jnp.int32, sums.shape, 1) // FACTOR_RANK
        query = jnp.full(sums.shape, -1, jnp.int32)
        block = jnp.full(sums.shape, -1, jnp.int32)
        for number in range(sums.shape[0] // QUERY_BLOCK):
            inside = (row // QUERY_BLOCK == number) & (count[0] > number)
            query = jnp.where(inside, pairs[0, number] * QUERY_BLOCK + row % QUERY_BLOCK, query)
            block = jnp.where(inside, pairs[1, number], block)
        picked = jnp.zeros_like(sums)
        for number in range(sums.shape[0]):
            picked = jnp.where(query == number, sums[number:number + 1], picked)
        column = lax.broadcasted_iota(jnp.int32, result_ref.shape, 1)
        result = jnp.zeros(result_ref.shape, jnp.float32)
        for d in range(DOC_BLOCK):
            value = jnp.sum(
                jnp.where(doc == block * DOC_BLOCK + d, picked, 0.0), axis=1, keepdims=True
            )
            result = jnp.where(column == d, value, result)
        result_ref[...] = result


def slot_scores(scalars, own, query_side, doc_side, doc_rows, eigen, spread, rest=()):
    model, queries = query_side.shape
    docs = doc_side.shape[1]
    last = bool(rest)
    padded = doc_rows.shape[1]
    bands = max(spread) + 1
    band = sum(rows.shape[0] for rows, place in zip(eigen, spread) if place == 0)
    lanes = queries if last else queries // 2
    out_rows = queries // FACTOR_RANK
    whole = lambda array: pl.BlockSpec(array.shape, lambda j, *_: (0, 0))
    in_specs = [whole(array) for array in (own, *rest)] + [
        pl.BlockSpec((band, lanes), lambda j, *_: (j, 0)),
        pl.BlockSpec((band, docs), lambda j, *_: (j, 0)),
        whole(doc_rows),
    ] + [pl.BlockSpec(memory_space=pl.ANY)] * len(eigen)
    shape = (out_rows, LANES if last else docs)
    scratch = [
        pltpu.VMEM((2, band, padded), jnp.bfloat16),
        pltpu.VMEM((2 * QUERY_BLOCK * band, padded), jnp.bfloat16),
        pltpu.VMEM((out_rows, docs), jnp.float32),
        pltpu.SemaphoreType.DMA((len(eigen),)),
    ]
    if last:
        scratch.append(pltpu.VMEM((queries, padded), jnp.bfloat16))
    return pl.pallas_call(
        lambda *refs: score_kernel(*refs, spread=spread, last=last),
        out_shape=jax.ShapeDtypeStruct(shape, jnp.float32),
        grid_spec=pltpu.PrefetchScalarGridSpec(
            num_scalar_prefetch=len(scalars),
            grid=(bands,),
            in_specs=in_specs,
            out_specs=pl.BlockSpec(shape, lambda j, *_: (0, 0)),
            scratch_shapes=scratch,
        ),
        compiler_params=pltpu.CompilerParams(
            dimension_semantics=("arbitrary",), vmem_limit_bytes=40 * 2**20
        ),
        cost_estimate=pl.CostEstimate(
            flops=2 * 2 * 2 * QUERY_BLOCK * bands * band * queries * padded,
            bytes_accessed=4 * bands * band * padded + 4 * 2**20, transcendentals=0,
        ),
    )(*scalars, own, *rest, query_side, doc_side, doc_rows, *eigen)


def local(
    query_out, query_in, basis_out, basis_in, eigenvalues, doc_out, doc_in, pair_list, pair_count
):
    layer, query, doc = (lax.axis_index(axis) for axis in ("layer", "query", "doc"))
    parts = lax.axis_size("doc")
    core = layer % 2
    odd = query % 2
    y, x = doc // SIDE, doc % SIDE
    model = doc_in.shape[2]

    def shift(array, by, first):
        pairs = []
        for source in range(lax.axis_size("layer") * parts):
            at, (row, column) = source // parts, divmod(source % parts, SIDE)
            if (at % 2 == 0) == first:
                column = (column + by) % SIDE
            else:
                row = (row + by) % SIDE
            pairs.append((source, at * parts + row * SIDE + column))
        return lax.ppermute(array, ("layer", "doc"), pairs)

    here = jnp.stack([odd, core, y, x]).astype(jnp.int32)
    scalars = (pair_list.T, pair_count, here)
    tail = -eigenvalues.shape[0] % TILE
    own_rows = eigenvalues.T
    left, right, across = (shift(own_rows, by, True) for by in (1, -1, 2))
    merge = lambda *rows: jnp.pad(
        jnp.concatenate(rows, axis=0), ((0, 0), (0, tail)), constant_values=1
    )
    top, bottom = merge(own_rows, left), merge(right, across)

    half = query_out.shape[0] // 2
    share = half // parts
    part_in = jnp.dot(
        lax.dynamic_slice_in_dim(query_in, core * half, half, 0), basis_in,
        preferred_element_type=jnp.float32,
    )
    part_out = jnp.dot(
        lax.dynamic_slice_in_dim(query_out, odd * half, half, 0), basis_out,
        preferred_element_type=jnp.float32,
    )
    partial = jnp.concatenate([part_in, jnp.pad(part_out, ((0, 0), (0, tail)))], axis=1)
    width = partial.shape[1]
    sent = (partial * SCALE).astype(jnp.float16).reshape(parts, share, width)
    received = lax.all_to_all(sent, "doc", 0, 0)
    summed = (jnp.sum(received.astype(jnp.float32), axis=0) * (1.0 / SCALE)).astype(jnp.bfloat16)

    doc_rows = jnp.pad(doc_out.reshape(-1, doc_out.shape[2]), ((0, 0), (0, tail)))
    in_rows = doc_in.reshape(-1, model)
    doc_side = arrange(here, in_rows, in_rows, lambda i, _: (0, 0), lambda i, _: (1, 0), model, False)
    after = [shift(rows, 1, False) for rows in (top, bottom)]
    before = [shift(rows, -1, False) for rows in (top, bottom)]

    copies = jnp.broadcast_to(summed[None], (parts, share, width))
    own = lax.all_to_all(copies, "doc", 0, 0).reshape(half, width)
    swap = lambda axis: [(i, i ^ 1) for i in range(lax.axis_size(axis))]
    far_out = lax.ppermute(own[:, model:], "query", swap("query"))
    far_in = lax.ppermute(own[:, :model], "layer", swap("layer"))

    last = [shift(after[0], 1, False), shift(before[1], -1, False)]
    eigen = [top, bottom, *after, *before, *last]
    spread = tuple(number // 2 for number in range(len(eigen)))
    query_side = arrange(here, own, far_in, lambda i, _: (0, 0), lambda i, _: (0, 0), model, True)
    sums = slot_scores(scalars, own, query_side, doc_side, doc_rows, eigen[:-2], spread[:-2])
    scores = slot_scores(
        scalars, own, query_side, doc_side, doc_rows, eigen, spread, (far_out, sums)
    )
    group = lax.axis_size("layer") * lax.axis_size("query")
    copies = jnp.broadcast_to(scores[None], (group,) + scores.shape)
    total = jnp.sum(lax.all_to_all(copies, ("layer", "query"), 0, 0), axis=0)
    return total[:, :DOC_BLOCK].reshape(pair_list.shape[0], QUERY_BLOCK * DOC_BLOCK)


def solution(mesh):
    in_specs = (
        P(None, "doc"),
        P(None, "doc"),
        P("doc", "layer"),
        P("doc", "query"),
        P("layer", ("query", "doc")),
        P("doc", None, "layer"),
        P("doc", None, "query"),
        P("doc", None),
        P("doc"),
    )
    out_specs = P("doc", None)
    return jax.shard_map(local, mesh=mesh, in_specs=in_specs, out_specs=out_specs, check_vma=False)
```

```python
import jax
import jax.numpy as jnp
from jax import lax
from jax.experimental import pallas as pl
from jax.experimental.pallas import tpu as pltpu
from jax.sharding import PartitionSpec as P

FACTOR_RANK = 32
QUERY_BLOCK = 2
DOC_BLOCK = 2
TILE = 256
CHUNK = 1536
LANES = 128
SIDE = 4
SCALE = 4096.0

damping = 0.1

ODD, CORE, ROW, COLUMN = range(4)
STEPS = (0, SIDE - 1, 1, 2)


def arrange_kernel(here, low_ref, high_ref, rows_ref, columns, *, swap):
    low = low_ref[...].astype(jnp.float32).T
    high = high_ref[...].astype(jnp.float32).T
    half = low.shape[1]
    if swap:
        keep = here[ODD] == here[CORE]
        low, high = jnp.where(keep, low, high), jnp.where(keep, high, low)
    columns[:, :half] = low
    columns[:, half:] = high
    size = columns.shape[0] // (SIDE * SIDE)
    first = here[CORE] == 0
    for outer in range(SIDE):
        for inner in range(SIDE):
            row = lax.rem(here[ROW] + jnp.where(first, STEPS[outer], STEPS[inner]), SIDE)
            column = lax.rem(here[COLUMN] + jnp.where(first, STEPS[inner], STEPS[outer]), SIDE)
            source = pl.multiple_of((row * SIDE + column) * size, size)
            place = (outer * SIDE + inner) * size
            rows_ref[place:place + size, :] = columns[pl.ds(source, size), :].astype(jnp.bfloat16)


def arrange(here, low, high, low_map, high_map, model, swap):
    half = 2 * FACTOR_RANK * QUERY_BLOCK
    return pl.pallas_call(
        lambda *refs: arrange_kernel(*refs, swap=swap),
        out_shape=jax.ShapeDtypeStruct((model, 2 * half), jnp.bfloat16),
        grid_spec=pltpu.PrefetchScalarGridSpec(
            num_scalar_prefetch=1,
            grid=(1,),
            in_specs=[pl.BlockSpec((half, model), low_map), pl.BlockSpec((half, model), high_map)],
            out_specs=pl.BlockSpec((model, 2 * half), lambda i, here: (0, 0)),
            scratch_shapes=[pltpu.VMEM((model, 2 * half), jnp.float32)],
        ),
        compiler_params=pltpu.CompilerParams(vmem_limit_bytes=32 * 2**20),
        cost_estimate=pl.CostEstimate(flops=0, bytes_accessed=4 * model * half * 2, transcendentals=0),
    )(here, low, high)


def score_kernel(pairs, count, here, *refs, spread, last):
    own_ref, refs = refs[0], refs[1:]
    if last:
        far_ref, earlier_ref, refs = refs[0], refs[1], refs[2:]
    query_ref, doc_ref, doc_rows_ref = refs[:3]
    eigen_refs = refs[3:3 + len(spread)]
    result_ref, eigen, scaled, total, sems = refs[3 + len(spread):8 + len(spread)]
    step = pl.program_id(0)
    padded = doc_rows_ref.shape[1]
    first = own_ref.shape[1] - padded
    band = eigen.shape[1]
    bands = max(spread) + 1
    slots = pairs.shape[1]
    blocks = total.shape[0] // QUERY_BLOCK
    if last:
        rows, first, half = refs[-1], 0, own_ref.shape[0]
        begin_place = jnp.where(step < bands - 1, blocks // 2, 0)
        end_place = blocks
    else:
        rows, begin_place, end_place = own_ref, 0, blocks // 2

    def fetch(which, start):
        offset = 0
        for number, place in enumerate(spread):
            if place == which:
                size = eigen_refs[number].shape[0]
                copy = pltpu.make_async_copy(
                    eigen_refs[number], eigen.at[which % 2, pl.ds(offset, size)], sems.at[number]
                )
                copy.start() if start else copy.wait()
                offset += size

    @pl.when(step == 0)
    def _():
        fetch(0, True)
        if last:
            total[...] = earlier_ref[...]
            rows[:half] = own_ref[:, own_ref.shape[1] - padded:]
            rows[half:] = far_ref[...]
        else:
            total[...] = jnp.zeros_like(total)

    for which in range(bands):
        @pl.when(step == which)
        def _():
            fetch(which, False)
            if which + 1 < bands:
                fetch(which + 1, True)

    arrived = lax.rem(step, 2)
    query_side = query_ref[...]
    doc_side = doc_ref[...].astype(jnp.float32)
    lane = lax.broadcasted_iota(jnp.int32, query_side.shape, 1) // FACTOR_RANK
    empty = jnp.zeros_like(query_side)

    def score(places):
        left = jnp.concatenate(
            [
                jnp.where(lane == place * QUERY_BLOCK + q, query_side, empty)
                for place in places for q in range(QUERY_BLOCK)
            ],
            axis=0,
        )
        parts = len(places) * QUERY_BLOCK
        mixed = None
        for begin in range(0, padded, TILE):
            end = begin + TILE
            product = jnp.dot(
                left, rows[:, first + begin:first + end], preferred_element_type=jnp.float32
            )
            shifted = eigen[arrived, :, begin:end].astype(jnp.float32) + damping
            guess = pl.reciprocal(shifted, approx=True)
            weights = guess * (2.0 - shifted * guess)
            for q in range(parts):
                part = slice(q * band, (q + 1) * band)
                scaled[part, begin:end] = (product[part] * weights).astype(jnp.bfloat16)
            if end % CHUNK == 0 or end == padded:
                chunk = slice((end - 1) // CHUNK * CHUNK, end)
                more = lax.dot_general(
                    scaled[:parts * band, chunk], doc_rows_ref[:, chunk], (((1,), (1,)), ((), ())),
                    preferred_element_type=jnp.float32,
                )
                mixed = more if mixed is None else mixed + more
        for q in range(parts):
            part = mixed[q * band:(q + 1) * band] * doc_side
            block = lax.rem(places[q // QUERY_BLOCK] + here[ODD] * (blocks // 2), blocks)
            row = block * QUERY_BLOCK + q % QUERY_BLOCK
            total[pl.ds(row, 1), :] += jnp.sum(part, axis=0, keepdims=True)

    def wanted(place):
        block = lax.rem(place + here[ODD] * (blocks // 2), blocks)
        found = jnp.bool_(False)
        for slot in range(slots):
            found = found | ((pairs[0, slot] == block) & (count[0] > slot))
        return found

    @pl.loop(begin_place // 2, end_place // 2)
    def _(pair):
        lower, upper = wanted(2 * pair), wanted(2 * pair + 1)

        @pl.when(lower & upper)
        def _():
            score((2 * pair, 2 * pair + 1))

        @pl.when(lower != upper)
        def _():
            score((2 * pair + jnp.where(upper, 1, 0),))

    @pl.when(step == bands - 1)
    def _():
        if not last:
            result_ref[...] = total[...]
            return
        sums = total[...]
        row = lax.broadcasted_iota(jnp.int32, sums.shape, 0)
        doc = lax.broadcasted_iota(jnp.int32, sums.shape, 1) // FACTOR_RANK
        query = jnp.full(sums.shape, -1, jnp.int32)
        block = jnp.full(sums.shape, -1, jnp.int32)
        for number in range(sums.shape[0] // QUERY_BLOCK):
            inside = (row // QUERY_BLOCK == number) & (count[0] > number)
            query = jnp.where(inside, pairs[0, number] * QUERY_BLOCK + row % QUERY_BLOCK, query)
            block = jnp.where(inside, pairs[1, number], block)
        picked = jnp.zeros_like(sums)
        for number in range(sums.shape[0]):
            picked = jnp.where(query == number, sums[number:number + 1], picked)
        column = lax.broadcasted_iota(jnp.int32, result_ref.shape, 1)
        result = jnp.zeros(result_ref.shape, jnp.float32)
        for d in range(DOC_BLOCK):
            value = jnp.sum(
                jnp.where(doc == block * DOC_BLOCK + d, picked, 0.0), axis=1, keepdims=True
            )
            result = jnp.where(column == d, value, result)
        result_ref[...] = result


def slot_scores(scalars, own, query_side, doc_side, doc_rows, eigen, spread, rest=()):
    model, queries = query_side.shape
    docs = doc_side.shape[1]
    last = bool(rest)
    padded = doc_rows.shape[1]
    bands = max(spread) + 1
    band = sum(rows.shape[0] for rows, place in zip(eigen, spread) if place == 0)
    lanes = queries if last else queries // 2
    out_rows = queries // FACTOR_RANK
    whole = lambda array: pl.BlockSpec(array.shape, lambda j, *_: (0, 0))
    in_specs = [whole(array) for array in (own, *rest)] + [
        pl.BlockSpec((band, lanes), lambda j, *_: (j, 0)),
        pl.BlockSpec((band, docs), lambda j, *_: (j, 0)),
        whole(doc_rows),
    ] + [pl.BlockSpec(memory_space=pl.ANY)] * len(eigen)
    shape = (out_rows, LANES if last else docs)
    scratch = [
        pltpu.VMEM((2, band, padded), jnp.bfloat16),
        pltpu.VMEM((2 * QUERY_BLOCK * band, padded), jnp.bfloat16),
        pltpu.VMEM((out_rows, docs), jnp.float32),
        pltpu.SemaphoreType.DMA((len(eigen),)),
    ]
    if last:
        scratch.append(pltpu.VMEM((queries, padded), jnp.bfloat16))
    return pl.pallas_call(
        lambda *refs: score_kernel(*refs, spread=spread, last=last),
        out_shape=jax.ShapeDtypeStruct(shape, jnp.float32),
        grid_spec=pltpu.PrefetchScalarGridSpec(
            num_scalar_prefetch=len(scalars),
            grid=(bands,),
            in_specs=in_specs,
            out_specs=pl.BlockSpec(shape, lambda j, *_: (0, 0)),
            scratch_shapes=scratch,
        ),
        compiler_params=pltpu.CompilerParams(
            dimension_semantics=("arbitrary",), vmem_limit_bytes=40 * 2**20
        ),
        cost_estimate=pl.CostEstimate(
            flops=2 * 2 * 2 * QUERY_BLOCK * bands * band * queries * padded,
            bytes_accessed=4 * bands * band * padded + 4 * 2**20, transcendentals=0,
        ),
    )(*scalars, own, *rest, query_side, doc_side, doc_rows, *eigen)


def local(
    query_out, query_in, basis_out, basis_in, eigenvalues, doc_out, doc_in, pair_list, pair_count
):
    layer, query, doc = (lax.axis_index(axis) for axis in ("layer", "query", "doc"))
    parts = lax.axis_size("doc")
    core = layer % 2
    odd = query % 2
    y, x = doc // SIDE, doc % SIDE
    model = doc_in.shape[2]

    def shift(array, by, first):
        pairs = []
        for source in range(lax.axis_size("layer") * parts):
            at, (row, column) = source // parts, divmod(source % parts, SIDE)
            if (at % 2 == 0) == first:
                column = (column + by) % SIDE
            else:
                row = (row + by) % SIDE
            pairs.append((source, at * parts + row * SIDE + column))
        return lax.ppermute(array, ("layer", "doc"), pairs)

    here = jnp.stack([odd, core, y, x]).astype(jnp.int32)
    scalars = (pair_list.T, pair_count, here)
    tail = -eigenvalues.shape[0] % TILE
    own_rows = eigenvalues.T
    left, right, across = (shift(own_rows, by, True) for by in (1, -1, 2))
    merge = lambda *rows: jnp.pad(
        jnp.concatenate(rows, axis=0), ((0, 0), (0, tail)), constant_values=1
    )
    top, bottom = merge(own_rows, left), merge(right, across)

    half = query_out.shape[0] // 2
    share = half // parts
    part_in = jnp.dot(
        lax.dynamic_slice_in_dim(query_in, core * half, half, 0), basis_in,
        preferred_element_type=jnp.float32,
    )
    part_out = jnp.dot(
        lax.dynamic_slice_in_dim(query_out, odd * half, half, 0), basis_out,
        preferred_element_type=jnp.float32,
    )
    partial = jnp.concatenate([part_in, jnp.pad(part_out, ((0, 0), (0, tail)))], axis=1)
    width = partial.shape[1]
    sent = (partial * SCALE).astype(jnp.float16).reshape(parts, share, width)
    received = lax.all_to_all(sent, "doc", 0, 0)
    summed = (jnp.sum(received.astype(jnp.float32), axis=0) * (1.0 / SCALE)).astype(jnp.bfloat16)

    doc_rows = jnp.pad(doc_out.reshape(-1, doc_out.shape[2]), ((0, 0), (0, tail)))
    in_rows = doc_in.reshape(-1, model)
    doc_side = arrange(here, in_rows, in_rows, lambda i, _: (0, 0), lambda i, _: (1, 0), model, False)
    after = [shift(rows, 1, False) for rows in (top, bottom)]
    before = [shift(rows, -1, False) for rows in (top, bottom)]

    copies = jnp.broadcast_to(summed[None], (parts, share, width))
    own = lax.all_to_all(copies, "doc", 0, 0).reshape(half, width)
    swap = lambda axis: [(i, i ^ 1) for i in range(lax.axis_size(axis))]
    far_out = lax.ppermute(own[:, model:], "query", swap("query"))
    far_in = lax.ppermute(own[:, :model], "layer", swap("layer"))

    last = [shift(after[0], 1, False), shift(before[1], -1, False)]
    eigen = [top, bottom, *after, *before, *last]
    spread = tuple(number // 2 for number in range(len(eigen)))
    query_side = arrange(here, own, far_in, lambda i, _: (0, 0), lambda i, _: (0, 0), model, True)
    sums = slot_scores(scalars, own, query_side, doc_side, doc_rows, eigen[:-2], spread[:-2])
    scores = slot_scores(
        scalars, own, query_side, doc_side, doc_rows, eigen, spread, (far_out, sums)
    )
    group = lax.axis_size("layer") * lax.axis_size("query")
    copies = jnp.broadcast_to(scores[None], (group,) + scores.shape)
    total = jnp.sum(lax.all_to_all(copies, ("layer", "query"), 0, 0), axis=0)
    return total[:, :DOC_BLOCK].reshape(pair_list.shape[0], QUERY_BLOCK * DOC_BLOCK)


def solution(mesh):
    in_specs = (
        P(None, "doc"),
        P(None, "doc"),
        P("doc", "layer"),
        P("doc", "query"),
        P("layer", ("query", "doc")),
        P("doc", None, "layer"),
        P("doc", None, "query"),
        P("doc", None),
        P("doc"),
    )
    out_specs = P("doc", None)
    return jax.shard_map(local, mesh=mesh, in_specs=in_specs, out_specs=out_specs, check_vma=False)
```

```python
import jax
import jax.numpy as jnp
from jax import lax
from jax.experimental import pallas as pl
from jax.experimental.pallas import tpu as pltpu
from jax.sharding import PartitionSpec as P

FACTOR_RANK = 32
QUERY_BLOCK = 2
DOC_BLOCK = 2
TILE = 256
LANES = 128
SIDE = 4
SCALE = 4096.0

damping = 0.1

ODD, CORE, ROW, COLUMN = range(4)
STEPS = (0, SIDE - 1, 1, 2)


def arrange_kernel(here, low_ref, high_ref, rows_ref, columns, *, swap):
    low = low_ref[...].astype(jnp.float32).T
    high = high_ref[...].astype(jnp.float32).T
    half = low.shape[1]
    if swap:
        keep = here[ODD] == here[CORE]
        low, high = jnp.where(keep, low, high), jnp.where(keep, high, low)
    columns[:, :half] = low
    columns[:, half:] = high
    size = columns.shape[0] // (SIDE * SIDE)
    first = here[CORE] == 0
    for outer in range(SIDE):
        for inner in range(SIDE):
            row = lax.rem(here[ROW] + jnp.where(first, STEPS[outer], STEPS[inner]), SIDE)
            column = lax.rem(here[COLUMN] + jnp.where(first, STEPS[inner], STEPS[outer]), SIDE)
            source = pl.multiple_of((row * SIDE + column) * size, size)
            place = (outer * SIDE + inner) * size
            rows_ref[place:place + size, :] = columns[pl.ds(source, size), :].astype(jnp.bfloat16)


def arrange(here, low, high, low_map, high_map, model, swap):
    half = 2 * FACTOR_RANK * QUERY_BLOCK
    return pl.pallas_call(
        lambda *refs: arrange_kernel(*refs, swap=swap),
        out_shape=jax.ShapeDtypeStruct((model, 2 * half), jnp.bfloat16),
        grid_spec=pltpu.PrefetchScalarGridSpec(
            num_scalar_prefetch=1,
            grid=(1,),
            in_specs=[pl.BlockSpec((half, model), low_map), pl.BlockSpec((half, model), high_map)],
            out_specs=pl.BlockSpec((model, 2 * half), lambda i, here: (0, 0)),
            scratch_shapes=[pltpu.VMEM((model, 2 * half), jnp.float32)],
        ),
        compiler_params=pltpu.CompilerParams(vmem_limit_bytes=32 * 2**20),
        cost_estimate=pl.CostEstimate(flops=0, bytes_accessed=4 * model * half * 2, transcendentals=0),
    )(here, low, high)


def score_kernel(pairs, count, here, *refs, spread, last):
    own_ref, refs = refs[0], refs[1:]
    if last:
        far_ref, earlier_ref, refs = refs[0], refs[1], refs[2:]
    query_ref, doc_ref, doc_rows_ref = refs[:3]
    eigen_refs = refs[3:3 + len(spread)]
    result_ref, eigen, scaled, total, sems = refs[3 + len(spread):8 + len(spread)]
    step = pl.program_id(0)
    padded = doc_rows_ref.shape[1]
    first = own_ref.shape[1] - padded
    band = eigen.shape[1]
    bands = max(spread) + 1
    slots = pairs.shape[1]
    blocks = total.shape[0] // QUERY_BLOCK
    if last:
        rows, first, half = refs[-1], 0, own_ref.shape[0]
        begin_place = jnp.where(step < bands - 1, blocks // 2, 0)
        end_place = blocks
    else:
        rows, begin_place, end_place = own_ref, 0, blocks // 2

    def fetch(which, start):
        offset = 0
        for number, place in enumerate(spread):
            if place == which:
                size = eigen_refs[number].shape[0]
                copy = pltpu.make_async_copy(
                    eigen_refs[number], eigen.at[which % 2, pl.ds(offset, size)], sems.at[number]
                )
                copy.start() if start else copy.wait()
                offset += size

    @pl.when(step == 0)
    def _():
        fetch(0, True)
        if last:
            total[...] = earlier_ref[...]
            rows[:half] = own_ref[:, own_ref.shape[1] - padded:]
            rows[half:] = far_ref[...]
        else:
            total[...] = jnp.zeros_like(total)

    for which in range(bands):
        @pl.when(step == which)
        def _():
            fetch(which, False)
            if which + 1 < bands:
                fetch(which + 1, True)

    arrived = lax.rem(step, 2)
    query_side = query_ref[...]
    doc_side = doc_ref[...].astype(jnp.float32)
    lane = lax.broadcasted_iota(jnp.int32, query_side.shape, 1) // FACTOR_RANK
    empty = jnp.zeros_like(query_side)

    def score(places):
        left = jnp.concatenate(
            [
                jnp.where(lane == place * QUERY_BLOCK + q, query_side, empty)
                for place in places for q in range(QUERY_BLOCK)
            ],
            axis=0,
        )
        parts = len(places) * QUERY_BLOCK
        for begin in range(0, padded, 2 * TILE):
            end = min(begin + 2 * TILE, padded)
            product = jnp.dot(
                left, rows[:, first + begin:first + end], preferred_element_type=jnp.float32
            )
            shifted = eigen[arrived, :, begin:end].astype(jnp.float32) + damping
            guess = pl.reciprocal(shifted, approx=True)
            weights = guess * (2.0 - shifted * guess)
            for q in range(parts):
                part = slice(q * band, (q + 1) * band)
                scaled[part, begin:end] = (product[part] * weights).astype(jnp.bfloat16)
        mixed = lax.dot_general(
            scaled[:parts * band], doc_rows_ref[...], (((1,), (1,)), ((), ())),
            preferred_element_type=jnp.float32,
        )
        for q in range(parts):
            part = mixed[q * band:(q + 1) * band] * doc_side
            block = lax.rem(places[q // QUERY_BLOCK] + here[ODD] * (blocks // 2), blocks)
            row = block * QUERY_BLOCK + q % QUERY_BLOCK
            total[pl.ds(row, 1), :] += jnp.sum(part, axis=0, keepdims=True)

    def wanted(place):
        block = lax.rem(place + here[ODD] * (blocks // 2), blocks)
        found = jnp.bool_(False)
        for slot in range(slots):
            found = found | ((pairs[0, slot] == block) & (count[0] > slot))
        return found

    @pl.loop(begin_place // 2, end_place // 2)
    def _(pair):
        lower, upper = wanted(2 * pair), wanted(2 * pair + 1)

        @pl.when(lower & upper)
        def _():
            score((2 * pair, 2 * pair + 1))

        @pl.when(lower != upper)
        def _():
            score((2 * pair + jnp.where(upper, 1, 0),))

    @pl.when(step == bands - 1)
    def _():
        if not last:
            result_ref[...] = total[...]
            return
        sums = total[...]
        row = lax.broadcasted_iota(jnp.int32, sums.shape, 0)
        doc = lax.broadcasted_iota(jnp.int32, sums.shape, 1) // FACTOR_RANK
        query = jnp.full(sums.shape, -1, jnp.int32)
        block = jnp.full(sums.shape, -1, jnp.int32)
        for number in range(sums.shape[0] // QUERY_BLOCK):
            inside = (row // QUERY_BLOCK == number) & (count[0] > number)
            query = jnp.where(inside, pairs[0, number] * QUERY_BLOCK + row % QUERY_BLOCK, query)
            block = jnp.where(inside, pairs[1, number], block)
        picked = jnp.zeros_like(sums)
        for number in range(sums.shape[0]):
            picked = jnp.where(query == number, sums[number:number + 1], picked)
        column = lax.broadcasted_iota(jnp.int32, result_ref.shape, 1)
        result = jnp.zeros(result_ref.shape, jnp.float32)
        for d in range(DOC_BLOCK):
            value = jnp.sum(
                jnp.where(doc == block * DOC_BLOCK + d, picked, 0.0), axis=1, keepdims=True
            )
            result = jnp.where(column == d, value, result)
        result_ref[...] = result


def slot_scores(scalars, own, query_side, doc_side, doc_rows, eigen, spread, rest=()):
    model, queries = query_side.shape
    docs = doc_side.shape[1]
    last = bool(rest)
    padded = doc_rows.shape[1]
    bands = max(spread) + 1
    band = sum(rows.shape[0] for rows, place in zip(eigen, spread) if place == 0)
    lanes = queries if last else queries // 2
    out_rows = queries // FACTOR_RANK
    whole = lambda array: pl.BlockSpec(array.shape, lambda j, *_: (0, 0))
    in_specs = [whole(array) for array in (own, *rest)] + [
        pl.BlockSpec((band, lanes), lambda j, *_: (j, 0)),
        pl.BlockSpec((band, docs), lambda j, *_: (j, 0)),
        whole(doc_rows),
    ] + [pl.BlockSpec(memory_space=pl.ANY)] * len(eigen)
    shape = (out_rows, LANES if last else docs)
    scratch = [
        pltpu.VMEM((2, band, padded), jnp.bfloat16),
        pltpu.VMEM((2 * QUERY_BLOCK * band, padded), jnp.bfloat16),
        pltpu.VMEM((out_rows, docs), jnp.float32),
        pltpu.SemaphoreType.DMA((len(eigen),)),
    ]
    if last:
        scratch.append(pltpu.VMEM((queries, padded), jnp.bfloat16))
    return pl.pallas_call(
        lambda *refs: score_kernel(*refs, spread=spread, last=last),
        out_shape=jax.ShapeDtypeStruct(shape, jnp.float32),
        grid_spec=pltpu.PrefetchScalarGridSpec(
            num_scalar_prefetch=len(scalars),
            grid=(bands,),
            in_specs=in_specs,
            out_specs=pl.BlockSpec(shape, lambda j, *_: (0, 0)),
            scratch_shapes=scratch,
        ),
        compiler_params=pltpu.CompilerParams(
            dimension_semantics=("arbitrary",), vmem_limit_bytes=40 * 2**20
        ),
        cost_estimate=pl.CostEstimate(
            flops=2 * 2 * 2 * QUERY_BLOCK * bands * band * queries * padded,
            bytes_accessed=4 * bands * band * padded + 4 * 2**20, transcendentals=0,
        ),
    )(*scalars, own, *rest, query_side, doc_side, doc_rows, *eigen)


def local(
    query_out, query_in, basis_out, basis_in, eigenvalues, doc_out, doc_in, pair_list, pair_count
):
    layer, query, doc = (lax.axis_index(axis) for axis in ("layer", "query", "doc"))
    parts = lax.axis_size("doc")
    core = layer % 2
    odd = query % 2
    y, x = doc // SIDE, doc % SIDE
    model = doc_in.shape[2]

    def shift(array, by, first):
        pairs = []
        for source in range(lax.axis_size("layer") * parts):
            at, (row, column) = source // parts, divmod(source % parts, SIDE)
            if (at % 2 == 0) == first:
                column = (column + by) % SIDE
            else:
                row = (row + by) % SIDE
            pairs.append((source, at * parts + row * SIDE + column))
        return lax.ppermute(array, ("layer", "doc"), pairs)

    here = jnp.stack([odd, core, y, x]).astype(jnp.int32)
    scalars = (pair_list.T, pair_count, here)
    tail = -eigenvalues.shape[0] % TILE
    own_rows = eigenvalues.T
    left, right, across = (shift(own_rows, by, True) for by in (1, -1, 2))
    merge = lambda *rows: jnp.pad(
        jnp.concatenate(rows, axis=0), ((0, 0), (0, tail)), constant_values=1
    )
    top, bottom = merge(own_rows, left), merge(right, across)

    half = query_out.shape[0] // 2
    share = half // parts
    part_in = jnp.dot(
        lax.dynamic_slice_in_dim(query_in, core * half, half, 0), basis_in,
        preferred_element_type=jnp.float32,
    )
    part_out = jnp.dot(
        lax.dynamic_slice_in_dim(query_out, odd * half, half, 0), basis_out,
        preferred_element_type=jnp.float32,
    )
    partial = jnp.concatenate([part_in, jnp.pad(part_out, ((0, 0), (0, tail)))], axis=1)
    width = partial.shape[1]
    sent = (partial * SCALE).astype(jnp.float16).reshape(parts, share, width)
    received = lax.all_to_all(sent, "doc", 0, 0)
    summed = (jnp.sum(received.astype(jnp.float32), axis=0) * (1.0 / SCALE)).astype(jnp.bfloat16)

    doc_rows = jnp.pad(doc_out.reshape(-1, doc_out.shape[2]), ((0, 0), (0, tail)))
    in_rows = doc_in.reshape(-1, model)
    doc_side = arrange(here, in_rows, in_rows, lambda i, _: (0, 0), lambda i, _: (1, 0), model, False)
    after = [shift(rows, 1, False) for rows in (top, bottom)]
    before = [shift(rows, -1, False) for rows in (top, bottom)]

    copies = jnp.broadcast_to(summed[None], (parts, share, width))
    own = lax.all_to_all(copies, "doc", 0, 0).reshape(half, width)
    swap = lambda axis: [(i, i ^ 1) for i in range(lax.axis_size(axis))]
    far_out = lax.ppermute(own[:, model:], "query", swap("query"))
    far_in = lax.ppermute(own[:, :model], "layer", swap("layer"))

    last = [shift(after[0], 1, False), shift(before[1], -1, False)]
    eigen = [top, bottom, *after, *before, *last]
    spread = tuple(number // 2 for number in range(len(eigen)))
    query_side = arrange(here, own, far_in, lambda i, _: (0, 0), lambda i, _: (0, 0), model, True)
    sums = slot_scores(scalars, own, query_side, doc_side, doc_rows, eigen[:-2], spread[:-2])
    scores = slot_scores(
        scalars, own, query_side, doc_side, doc_rows, eigen, spread, (far_out, sums)
    )
    group = lax.axis_size("layer") * lax.axis_size("query")
    copies = jnp.broadcast_to(scores[None], (group,) + scores.shape)
    total = jnp.sum(lax.all_to_all(copies, ("layer", "query"), 0, 0), axis=0)
    return total[:, :DOC_BLOCK].reshape(pair_list.shape[0], QUERY_BLOCK * DOC_BLOCK)


def solution(mesh):
    in_specs = (
        P(None, "doc"),
        P(None, "doc"),
        P("doc", "layer"),
        P("doc", "query"),
        P("layer", ("query", "doc")),
        P("doc", None, "layer"),
        P("doc", None, "query"),
        P("doc", None),
        P("doc"),
    )
    out_specs = P("doc", None)
    return jax.shard_map(local, mesh=mesh, in_specs=in_specs, out_specs=out_specs, check_vma=False)
```
